32 devices in a mesh: dp: 8 (over z, x), tensor: 4 (over y, core).
Axes of the slice: x: 2, y: 2, z: 4, core: 2. Of those that a mesh axis runs over, the one named last changes fastest.
Arguments:
- inputs: bfloat16 [4096, 768], P(('dp', 'tensor')), may hold values from -6 to 6
- segment_ids: int32 [8, 512], P('dp'), may hold values from 0 to 3, never falling along the last dimension, each value on 1 to 256 neighbouring positions
- gain_attn: float32 [768], replicated, may hold values from 0.5 to 1.5
- gain_ffn: float32 [768], replicated, may hold values from 0.5 to 1.5
- query_key_value_weight: bfloat16 [768, 3, 768], P('dp', None, 'tensor'), may hold values from -1 to 1
- w_out: bfloat16 [768, 768], P('dp', 'tensor'), may hold values from -1.75 to 1.75
- w_ffn_in: bfloat16 [768, 2, 1152], P('dp', None, 'tensor'), may hold values from -0.21875 to 0.21875
- w_ffn_out: bfloat16 [768, 1152], P('dp', 'tensor'), may hold values from -0.1875 to 0.1875
- cotangent: bfloat16 [4096, 768], P(('dp', 'tensor')), may hold values from -6 to 6
Outputs:
- output: bfloat16 [4096, 768], P(('dp', 'tensor'))
- input_grad: float32 [4096, 768], P(('dp', 'tensor'))
- gain_attn_grad: float32 [768], replicated
- gain_ffn_grad: float32 [768], replicated
- w_qkv_grad: float32 [768, 3, 768], P('dp', None, 'tensor')
- w_out_grad: float32 [768, 768], P('dp', 'tensor')
- w_ffn_in_grad: float32 [768, 2, 1152], P('dp', None, 'tensor')
- w_ffn_out_grad: float32 [768, 1152], P('dp', 'tensor')
The draws below stay inside these ranges and needn't reach their ends.
Inputs may be any that keep to these rules, and one draw needn't show every extreme that they name: `segment_ids`: each row holds the sequence numbers of one data group's 512 tokens: 4 whole sequences laid end to end, numbers never falling, each sequence 1 to 256 tokens long and one exactly 256.
All inputs are finite; a program needn't handle non-finite values.
Results may differ from the reference program's by a relative error of at most 0.013.
Values may be sent and summed in bfloat16 or wider, within the bound.
A program may use at most 64 MiB of HBM per device.

```python
import math
import jax
import jax.numpy as jnp
import numpy as np
from jax import lax

D = 768
HD = 64
FF = 1152
TOK_DEV = 512
SEQS = 4
LMAX = 256
TOKENS = 4096
N_DP = 8


def draw_query_key_value_weight(key, part):
    scale_in = D ** (-0.5)
    return jnp.clip(jax.random.normal(key, (D, 3, D), jnp.float32) * scale_in, -1.0, 1.0).astype(jnp.bfloat16)


def block_levels(stream_key, extent, cuts, smallest, top_value):
    level, own = 1.0, jax.random.fold_in(stream_key, 6)
    for axis_at, shards_of in cuts:
        heights = jnp.exp(jax.random.uniform(jax.random.fold_in(own, axis_at), (shards_of,), jnp.float32, smallest / len(cuts), top_value / len(cuts)))
        level = level * jnp.repeat(heights, extent[axis_at] // shards_of).reshape([-1 if axis == axis_at else 1 for axis in range(len(extent))])
    return level


def profile(count, total, limit, lean):
    portions = [(1 << 20) // math.isqrt(rank ** lean) + 1 for rank in range(2, count + 1)]
    rest, holding = total - limit - (count - 1), [1] * (count - 1)
    while rest > 0:
        free = [i for i in range(count - 1) if holding[i] < limit]
        whole, budget = sum([portions[i] for i in free]), rest
        for i in free:
            more = min(limit - holding[i], max(1, budget * portions[i] // whole), rest)
            holding[i] = holding[i] + more
            rest = rest - more
    return np.array([limit] + holding)


def ragged(rng, count, total, most, slope):
    if count == 2:
        one = jax.random.randint(rng, (), max(1, total - most), min(most, total - 1) + 1)
        return jnp.stack([one, total - one])
    tallies = jnp.asarray(profile(count, total, most, slope), jnp.int32)
    couples = (count - 1) // 2
    source_of, taker = tallies[1:1 + 2 * couples:2], tallies[2:2 + 2 * couples:2]
    margin = jnp.minimum(source_of - 1, most - taker)
    passed = jax.random.randint(jax.random.fold_in(rng, 1), (couples,), 0, 1 << 20) % (margin + 1)
    tallies = tallies.at[1:1 + 2 * couples:2].set(source_of - passed).at[2:2 + 2 * couples:2].set(taker + passed)
    return tallies[jax.random.permutation(jax.random.fold_in(rng, 2), count)]


def bell_draw(rng, shape, scale, limit, split=(), kind=jnp.bfloat16):
    gain = block_levels(rng, shape, split, -0.22, 0.18) if split else 1.0
    values = jax.random.normal(rng, shape, jnp.float32) * scale * gain
    return jnp.minimum(jnp.maximum(values, -limit), limit).astype(kind)


def setup_inputs(seed: int = 0) -> dict:
    keys = jax.random.split(jax.random.key(seed), 10)
    inputs = bell_draw(keys[0], (TOKENS, D), 1.0, 6.0, ((0, 32),))
    segment_ids = jax.vmap(lambda own: jnp.searchsorted(jnp.cumsum(ragged(own, SEQS, TOK_DEV, LMAX, 2)), jnp.arange(TOK_DEV), side="right"))(jax.random.split(keys[1], N_DP)).reshape((N_DP, TOK_DEV)).astype(jnp.int32)
    gain_attn = jnp.clip(1.0 + 0.1 * jax.random.normal(keys[2], (D,), jnp.float32), 0.5, 1.5)
    gain_ffn = jnp.clip(1.0 + 0.1 * jax.random.normal(keys[3], (D,), jnp.float32), 0.5, 1.5)
    query_key_value_weight = draw_query_key_value_weight(jax.random.fold_in(keys[9], 71), 0)
    w_out = bell_draw(keys[5], (D, D), (D // 64) ** -0.5, 1.75, ((0, 8), (1, 4)))
    w_ffn_in = bell_draw(keys[6], (D, 2, FF), D ** -0.5, 0.21875, ((0, 8), (2, 4)))
    w_ffn_out = bell_draw(keys[7], (D, FF), FF ** -0.5, 0.1875, ((0, 8), (1, 4)))
    cotangent = bell_draw(keys[8], (TOKENS, D), 1.0, 6.0, ((0, 32),))
    return dict(inputs=inputs, segment_ids=segment_ids, gain_attn=gain_attn, gain_ffn=gain_ffn, query_key_value_weight=query_key_value_weight, w_out=w_out, w_ffn_in=w_ffn_in, w_ffn_out=w_ffn_out, cotangent=cotangent)


EPS = 1e-05
THETA = 160000.0

def normalize(row_data):
    centre = row_data - lax.optimization_barrier(jnp.mean(row_data, axis=-1, keepdims=True))
    inverse = lax.rsqrt(lax.optimization_barrier(jnp.mean(centre * centre, axis=-1, keepdims=True)) + EPS)
    return (centre * inverse, inverse)

def norm_back(grad_normed, unit_rows, inverse, gain_row):
    grad_unit = grad_normed * gain_row
    mean_grad = lax.optimization_barrier(jnp.mean(grad_unit, axis=-1, keepdims=True))
    mean_dot = lax.optimization_barrier(jnp.mean(grad_unit * unit_rows, axis=-1, keepdims=True))
    return inverse * (grad_unit - mean_grad - unit_rows * mean_dot)

def gelu_parts(values_in):
    normal_cdf = 0.5 * (1.0 + jax.scipy.special.erf(values_in * 0.7071067811865476))
    density = 0.3989422804014327 * jnp.exp(-0.5 * values_in * values_in)
    return (values_in * normal_cdf, normal_cdf + values_in * density)

def rotary_tables(segments, head_size):
    token_count = segments.shape[0]
    places = jnp.arange(token_count, dtype=jnp.int32)
    previous = jnp.concatenate([jnp.full((1,), -1, jnp.int32), segments[:-1]])
    starts = lax.cummax(jnp.where(segments != previous, places, 0), axis=0)
    position = (places - starts).astype(jnp.float32)
    half_size = head_size // 2
    exponent = -(2.0 * jnp.arange(half_size, dtype=jnp.float32)) / head_size
    frequency = jnp.power(jnp.float32(THETA), exponent)
    angles = position[:, None] * frequency[None, :]
    return (jnp.cos(angles), jnp.sin(angles))

def rotate(vectors, cosine, sine):
    half_size = vectors.shape[-1] // 2
    first_half = vectors[..., :half_size]
    second_half = vectors[..., half_size:]
    cos_part = cosine[:, None, :]
    sin_part = sine[:, None, :]
    return jnp.concatenate([first_half * cos_part - second_half * sin_part, second_half * cos_part + first_half * sin_part], axis=-1)

def block_scores(q_block, keyset, seg_block, segments, scale):
    scores = jnp.einsum('qhe,khe->hqk', q_block.astype(jnp.float32), keyset.astype(jnp.float32)) * scale
    same_seq = seg_block[:, None] == segments[None, :]
    return jnp.where(same_seq[None], scores, jnp.float32(-1e+30))

def attention_forward(query, keyset, valueset, segments, block):
    scale = query.shape[-1] ** (-0.5)
    out_list = []
    total_list = []
    for start in range(0, query.shape[0], block):
        scores = block_scores(query[start:start + block], keyset, segments[start:start + block], segments, scale)
        top_score = lax.optimization_barrier(jnp.max(scores, axis=-1, keepdims=True))
        log_total = top_score + jnp.log(lax.optimization_barrier(jnp.sum(jnp.exp(scores - top_score), axis=-1, keepdims=True)))
        probs = jnp.exp(scores - log_total).astype(jnp.bfloat16)
        out_block = jnp.einsum('hqk,khe->qhe', probs.astype(jnp.float32), valueset.astype(jnp.float32))
        out_list.append(out_block.astype(jnp.bfloat16))
        total_list.append(log_total)
    return (jnp.concatenate(out_list, axis=0), jnp.concatenate(total_list, axis=1))

def attention_backward(query, keyset, valueset, segments, heads_out, log_totals, grad_heads, block):
    scale = query.shape[-1] ** (-0.5)
    grad_keys = jnp.zeros(keyset.shape, jnp.float32)
    grad_values = jnp.zeros(valueset.shape, jnp.float32)
    query_list = []
    for start in range(0, query.shape[0], block):
        q_block = query[start:start + block]
        grad_block = grad_heads[start:start + block].astype(jnp.float32)
        out_block = heads_out[start:start + block].astype(jnp.float32)
        scores = block_scores(q_block, keyset, segments[start:start + block], segments, scale)
        probs_f = jnp.exp(scores - log_totals[:, start:start + block])
        probs = probs_f.astype(jnp.bfloat16).astype(jnp.float32)
        grad_values = grad_values + jnp.einsum('hqk,qhe->khe', probs, grad_block)
        grad_probs = jnp.einsum('qhe,khe->hqk', grad_block, valueset.astype(jnp.float32))
        row_dot = lax.optimization_barrier(jnp.sum(grad_block * out_block, axis=-1)).T[:, :, None]
        grad_scores = (probs_f * (grad_probs - row_dot)).astype(jnp.bfloat16).astype(jnp.float32)
        query_list.append(jnp.einsum('hqk,khe->qhe', grad_scores, keyset.astype(jnp.float32)) * scale)
        grad_keys = grad_keys + jnp.einsum('hqk,qhe->khe', grad_scores, q_block.astype(jnp.float32)) * scale
    return (jnp.concatenate(query_list, axis=0), grad_keys, grad_values)

def layer(x_rows, seg_row, cot_rows, gain_attn, gain_ffn, query_key_value_weight, w_out, w_ffn_in, w_ffn_out):
    token_count = x_rows.shape[0]
    block = min(512, token_count)
    resid_in = x_rows.astype(jnp.float32)
    unit_one, inv_one = normalize(resid_in)
    first_normed_rows = (unit_one * gain_attn).astype(jnp.bfloat16)
    attention_mixed = jnp.einsum('jk,knr->jnr', first_normed_rows.astype(jnp.float32), query_key_value_weight.astype(jnp.float32))
    cosine, sine = rotary_tables(seg_row, HD)
    query = rotate(attention_mixed[:, 0].reshape(token_count, -1, HD), cosine, sine).astype(jnp.bfloat16)
    keyset = rotate(attention_mixed[:, 1].reshape(token_count, -1, HD), cosine, sine).astype(jnp.bfloat16)
    valueset = attention_mixed[:, 2].reshape(token_count, -1, HD).astype(jnp.bfloat16)
    heads_out, log_totals = attention_forward(query, keyset, valueset, seg_row, block)
    flat_out = heads_out.reshape(token_count, -1)
    resid_mid = resid_in + jnp.dot(flat_out, w_out.T, preferred_element_type=jnp.float32)
    unit_two, inv_two = normalize(resid_mid)
    normed_two = (unit_two * gain_ffn).astype(jnp.bfloat16)
    gate_up = jnp.einsum('td,dsf->tsf', normed_two.astype(jnp.float32), w_ffn_in.astype(jnp.float32))
    gelu_val, gelu_slope = gelu_parts(gate_up[:, 0])
    hidden = (gelu_val * gate_up[:, 1]).astype(jnp.bfloat16)
    result = (resid_mid + jnp.dot(hidden, w_ffn_out.T, preferred_element_type=jnp.float32)).astype(jnp.bfloat16)
    down_grad = jnp.dot(cot_rows.T, hidden, preferred_element_type=jnp.float32)
    grad_hidden = jnp.dot(cot_rows, w_ffn_out, preferred_element_type=jnp.float32)
    grad_mix = jnp.stack([grad_hidden * gate_up[:, 1] * gelu_slope, grad_hidden * gelu_val], axis=1).astype(jnp.bfloat16)
    in_grad = jnp.einsum('td,tsf->dsf', normed_two.astype(jnp.float32), grad_mix.astype(jnp.float32))
    grad_two = jnp.einsum('tsf,dsf->td', grad_mix.astype(jnp.float32), w_ffn_in.astype(jnp.float32))
    gain_ffn_part = lax.optimization_barrier(jnp.sum(grad_two * unit_two, axis=0))
    grad_mid = cot_rows.astype(jnp.float32) + norm_back(grad_two, unit_two, inv_two, gain_ffn)
    grad_mid_b = grad_mid.astype(jnp.bfloat16)
    out_grad = jnp.dot(grad_mid_b.T, flat_out, preferred_element_type=jnp.float32)
    grad_heads = jnp.dot(grad_mid_b, w_out, preferred_element_type=jnp.float32).astype(jnp.bfloat16)
    grad_heads = grad_heads.reshape(token_count, -1, HD)
    grad_query, grad_keys, grad_values = attention_backward(query, keyset, valueset, seg_row, heads_out, log_totals, grad_heads, block)
    grad_query = rotate(grad_query, cosine, -sine)
    grad_keys = rotate(grad_keys, cosine, -sine)
    query_key_value_gradient = jnp.stack([grad_query.reshape(token_count, -1), grad_keys.reshape(token_count, -1), grad_values.reshape(token_count, -1)], axis=1).astype(jnp.bfloat16)
    gradient_query_key_value = jnp.einsum('hz,hjx->zjx', first_normed_rows.astype(jnp.float32), query_key_value_gradient.astype(jnp.float32))
    first_norm_gradient = jnp.einsum('bwi,uwi->bu', query_key_value_gradient.astype(jnp.float32), query_key_value_weight.astype(jnp.float32))
    gain_attn_part = lax.optimization_barrier(jnp.sum(first_norm_gradient * unit_one, axis=0))
    grad_input = grad_mid + norm_back(first_norm_gradient, unit_one, inv_one, gain_attn)
    return (result, grad_input, (gain_attn_part, gain_ffn_part, gradient_query_key_value, out_grad, in_grad, down_grad))

def reference(inputs, segment_ids, gain_attn, gain_ffn, query_key_value_weight, w_out, w_ffn_in, w_ffn_out, cotangent):
    groups = segment_ids.shape[0]
    span = segment_ids.shape[1]
    width = inputs.shape[1]
    x_all = inputs.reshape(groups, span, width)
    c_all = cotangent.reshape(groups, span, width)
    zeros = (jnp.zeros(gain_attn.shape, jnp.float32), jnp.zeros(gain_ffn.shape, jnp.float32), jnp.zeros(query_key_value_weight.shape, jnp.float32), jnp.zeros(w_out.shape, jnp.float32), jnp.zeros(w_ffn_in.shape, jnp.float32), jnp.zeros(w_ffn_out.shape, jnp.float32))

    def one_group(carry, pieces):
        x_rows, seg_row, cot_rows = pieces
        result, grad_input, grads = layer(x_rows, seg_row, cot_rows, gain_attn, gain_ffn, query_key_value_weight, w_out, w_ffn_in, w_ffn_out)
        return (tuple((total + piece for total, piece in zip(carry, grads))), (result, grad_input))
    totals, (results, grad_inputs) = lax.scan(one_group, zeros, (x_all, segment_ids, c_all))
    return (results.reshape(groups * span, width), grad_inputs.reshape(groups * span, width), totals[0], totals[1], totals[2], totals[3], totals[4], totals[5])
```

```python
import functools

import jax
import jax.numpy as jnp
import numpy as np
from jax import lax
from jax.experimental import pallas as pl
from jax.experimental.pallas import tpu as pltpu
from jax.sharding import PartitionSpec as P

HD = 64


EPS = 1e-05
THETA = 160000.0


def normalize(row_data):
    centre = row_data - jnp.mean(row_data, axis=-1, keepdims=True)
    inverse = lax.rsqrt(jnp.mean(centre * centre, axis=-1, keepdims=True) + EPS)
    return (centre * inverse, inverse)


def norm_back(grad_normed, unit_rows, inverse, gain_row):
    grad_unit = grad_normed * gain_row
    mean_grad = jnp.mean(grad_unit, axis=-1, keepdims=True)
    mean_dot = jnp.mean(grad_unit * unit_rows, axis=-1, keepdims=True)
    return inverse * (grad_unit - mean_grad - unit_rows * mean_dot)


def gelu_parts(values_in):
    normal_cdf = 0.5 * (1.0 + jax.scipy.special.erf(values_in * 0.7071067811865476))
    density = 0.3989422804014327 * jnp.exp(-0.5 * values_in * values_in)
    return (values_in * normal_cdf, normal_cdf + values_in * density)


def rotary_tables(segments, head_size):
    token_count = segments.shape[0]
    places = jnp.arange(token_count, dtype=jnp.int32)
    previous = jnp.concatenate([jnp.full((1,), -1, jnp.int32), segments[:-1]])
    starts = lax.cummax(jnp.where(segments != previous, places, 0), axis=0)
    position = (places - starts).astype(jnp.float32)
    half_size = head_size // 2
    exponent = -(2.0 * jnp.arange(half_size, dtype=jnp.float32)) / head_size
    frequency = jnp.power(jnp.float32(THETA), exponent)
    angles = position[:, None] * frequency[None, :]
    return (jnp.cos(angles), jnp.sin(angles))


def rotate(vectors, cosine, sine):
    half_size = vectors.shape[-1] // 2
    first_half = vectors[..., :half_size]
    second_half = vectors[..., half_size:]
    cos_part = cosine[:, None, :]
    sin_part = sine[:, None, :]
    return jnp.concatenate(
        [
            first_half * cos_part - second_half * sin_part,
            second_half * cos_part + first_half * sin_part,
        ],
        axis=-1,
    )


def block_scores(q_block, keyset, seg_block, segments, scale):
    scores = jnp.einsum("qhe,khe->hqk", q_block, keyset, preferred_element_type=jnp.float32) * scale
    same_seq = seg_block[:, None] == segments[None, :]
    return jnp.where(same_seq[None], scores, jnp.float32(-1e30))


def attention_forward(query, keyset, valueset, segments):
    scale = query.shape[-1] ** (-0.5)
    scores = block_scores(query, keyset, segments, segments, scale)
    top_score = jnp.max(scores, axis=-1, keepdims=True)
    log_total = top_score + jnp.log(jnp.sum(jnp.exp(scores - top_score), axis=-1, keepdims=True))
    probs = jnp.exp(scores - log_total).astype(jnp.bfloat16)
    out_block = jnp.einsum("hqk,khe->qhe", probs, valueset, preferred_element_type=jnp.float32)
    out_list = out_block.astype(jnp.bfloat16)
    return (out_list, log_total)


def attention_backward(query, keyset, valueset, segments, heads_out, log_totals, grad_heads):
    scale = query.shape[-1] ** (-0.5)
    scores = block_scores(query, keyset, segments, segments, scale)
    probs_f = jnp.exp(scores - log_totals)
    probs = probs_f.astype(jnp.bfloat16)
    grad_values = jnp.einsum("hqk,qhe->khe", probs, grad_heads, preferred_element_type=jnp.float32)
    grad_probs = jnp.einsum(
        "qhe,khe->hqk", grad_heads, valueset, preferred_element_type=jnp.float32
    )
    row_dot = jnp.sum(grad_heads.astype(jnp.float32) * heads_out.astype(jnp.float32), axis=-1).T[
        :, :, None
    ]
    grad_scores = (probs_f * (grad_probs - row_dot)).astype(jnp.bfloat16)
    query_list = (
        jnp.einsum("hqk,khe->qhe", grad_scores, keyset, preferred_element_type=jnp.float32) * scale
    )
    grad_keys = (
        jnp.einsum("hqk,qhe->khe", grad_scores, query, preferred_element_type=jnp.float32) * scale
    )
    return (query_list, grad_keys, grad_values)


def spread_rows(row_data):
    return lax.all_gather(row_data, "tensor", axis=0, tiled=True)


def merge_rows(partial_value):
    return lax.psum_scatter(partial_value, "tensor", scatter_dimension=0, tiled=True)


def spread_grads(row_data):
    return lax.all_gather(row_data, "tensor", axis=0, tiled=True)


def merge_grads(partial_value):
    return lax.psum_scatter(partial_value, "tensor", scatter_dimension=0, tiled=True)


def on_device(
    inputs,
    segment_ids,
    gain_attn,
    gain_ffn,
    query_key_value_weight,
    w_out,
    w_ffn_in,
    w_ffn_out,
    cotangent,
):
    query_key_value_full, full_out, full_in, full_down = (
        lax.all_gather(query_key_value_weight, "dp", axis=0, tiled=True),
        lax.all_gather(w_out, "dp", axis=0, tiled=True),
        lax.all_gather(w_ffn_in, "dp", axis=0, tiled=True),
        lax.all_gather(w_ffn_out, "dp", axis=0, tiled=True),
    )
    seg_row = segment_ids[0]
    token_count = seg_row.shape[0]
    contract_last = (((1,), (1,)), ((), ()))
    contract_first = (((0,), (0,)), ((), ()))
    resid_in = inputs.astype(jnp.float32)
    unit_one, inv_one = normalize(resid_in)
    first_normed_rows = spread_rows((unit_one * gain_attn).astype(jnp.bfloat16))
    attention_mixed = jnp.einsum(
        "jk,knr->jnr", first_normed_rows, query_key_value_full, preferred_element_type=jnp.float32
    )
    cosine, sine = rotary_tables(seg_row, HD)
    query = rotate(attention_mixed[:, 0].reshape(token_count, -1, HD), cosine, sine).astype(
        jnp.bfloat16
    )
    keyset = rotate(attention_mixed[:, 1].reshape(token_count, -1, HD), cosine, sine).astype(
        jnp.bfloat16
    )
    valueset = attention_mixed[:, 2].reshape(token_count, -1, HD).astype(jnp.bfloat16)
    heads_out, log_totals = attention_forward(query, keyset, valueset, seg_row)
    flat_out = heads_out.reshape(token_count, -1)
    attn_part = lax.dot_general(
        flat_out, full_out, contract_last, preferred_element_type=jnp.float32
    )
    resid_mid = resid_in + merge_rows(attn_part)
    unit_two, inv_two = normalize(resid_mid)
    normed_two = spread_rows((unit_two * gain_ffn).astype(jnp.bfloat16))
    gate_up = jnp.einsum("td,dsf->tsf", normed_two, full_in, preferred_element_type=jnp.float32)
    gelu_val, gelu_slope = gelu_parts(gate_up[:, 0])
    hidden = (gelu_val * gate_up[:, 1]).astype(jnp.bfloat16)
    ffn_part = lax.dot_general(hidden, full_down, contract_last, preferred_element_type=jnp.float32)
    result = (resid_mid + merge_rows(ffn_part)).astype(jnp.bfloat16)
    query_key_value_back, back_out, back_in, back_down = (
        query_key_value_full,
        full_out,
        full_in,
        full_down,
    )
    grad_top = spread_grads(cotangent)
    down_grad = lax.dot_general(
        grad_top, hidden, contract_first, preferred_element_type=jnp.float32
    )
    grad_hidden = jnp.dot(grad_top, back_down, preferred_element_type=jnp.float32)
    grad_mix = jnp.stack(
        [grad_hidden * gate_up[:, 1] * gelu_slope, grad_hidden * gelu_val], axis=1
    ).astype(jnp.bfloat16)
    in_grad = jnp.einsum("td,tsf->dsf", normed_two, grad_mix, preferred_element_type=jnp.float32)
    grad_two = merge_grads(
        jnp.einsum("tsf,dsf->td", grad_mix, back_in, preferred_element_type=jnp.float32)
    )
    gain_ffn_part = jnp.sum(grad_two * unit_two, axis=0)
    grad_mid = cotangent.astype(jnp.float32) + norm_back(grad_two, unit_two, inv_two, gain_ffn)
    grad_mid_full = spread_grads(grad_mid.astype(jnp.bfloat16))
    out_grad = lax.dot_general(
        grad_mid_full, flat_out, contract_first, preferred_element_type=jnp.float32
    )
    grad_heads = jnp.dot(grad_mid_full, back_out, preferred_element_type=jnp.float32).astype(
        jnp.bfloat16
    )
    grad_heads = grad_heads.reshape(token_count, -1, HD)
    grad_query, grad_keys, grad_values = attention_backward(
        query, keyset, valueset, seg_row, heads_out, log_totals, grad_heads
    )
    grad_query = rotate(grad_query, cosine, -sine)
    grad_keys = rotate(grad_keys, cosine, -sine)
    query_key_value_gradient = jnp.stack(
        [
            grad_query.reshape(token_count, -1),
            grad_keys.reshape(token_count, -1),
            grad_values.reshape(token_count, -1),
        ],
        axis=1,
    ).astype(jnp.bfloat16)
    gradient_query_key_value = jnp.einsum(
        "hz,hjx->zjx",
        first_normed_rows,
        query_key_value_gradient,
        preferred_element_type=jnp.float32,
    )
    first_norm_gradient = merge_grads(
        jnp.einsum(
            "bwi,uwi->bu",
            query_key_value_gradient,
            query_key_value_back,
            preferred_element_type=jnp.float32,
        )
    )
    gain_attn_part = jnp.sum(first_norm_gradient * unit_one, axis=0)
    grad_input = grad_mid + norm_back(first_norm_gradient, unit_one, inv_one, gain_attn)
    gain_attn_grad, gain_ffn_grad = lax.psum((gain_attn_part, gain_ffn_part), ("dp", "tensor"))
    qkv_share, out_share, in_share, down_share = (
        lax.psum_scatter(gradient_query_key_value, "dp", scatter_dimension=0, tiled=True),
        lax.psum_scatter(out_grad, "dp", scatter_dimension=0, tiled=True),
        lax.psum_scatter(in_grad, "dp", scatter_dimension=0, tiled=True),
        lax.psum_scatter(down_grad, "dp", scatter_dimension=0, tiled=True),
    )
    return (
        result,
        grad_input,
        gain_attn_grad,
        gain_ffn_grad,
        qkv_share,
        out_share,
        in_share,
        down_share,
    )


BF = jnp.bfloat16
F32 = jnp.float32
LAST = (((1,), (1,)), ((), ()))
FIRST = (((0,), (0,)), ((), ()))
PLAIN = (((1,), (0,)), ((), ()))


def dot(a, b, dims=PLAIN):
    return lax.dot_general(a, b, dims, preferred_element_type=F32)


def partner(chunk):
    lane = lax.broadcasted_iota(jnp.int32, chunk.shape, 1)
    return jnp.where(lane % 64 < 32, pltpu.roll(chunk, 96, 1), pltpu.roll(chunk, 32, 1))


def rms_parts(rows):
    centre = rows - jnp.mean(rows, axis=-1, keepdims=True)
    inverse = lax.rsqrt(jnp.mean(centre * centre, axis=-1, keepdims=True) + EPS)
    return centre * inverse, inverse


def fused_kernel(
    n_dp, n_t, n_head, ff,
    x_ref, cot_ref, seg_ref, gain1_ref, gain2_ref, freq_ref, a_ref, b_ref,
    out_ref, gin_ref, gains_ref, ga_ref, gb_ref,
    xg, cg, ag, bg, n1, n2g, gmg, cosb, sinb, bias, qkvh, probs, hoh, hof, wo, wg, wu, wd,
    rs1s, rs1r, rs2s, rs2r, rs3s, rs3r, rs4s, rs4r, own1, own2, own3, own4,
    ghf, hid, mix0, mix1, unit2, mid, gmid, ghh, dsb, dqkv, gq, ags, agr, bgs, bgr, gpt, gpd,
    t_send, t_recv, d_send, d_recv,
):
    d = lax.axis_index("dp")
    t = lax.axis_index("tensor")
    rows, width = x_ref.shape
    wrows = a_ref.shape[0]
    head_cols = n_head * HD
    qkv_cols = 3 * head_cols
    span = n_t * rows

    barrier = pltpu.get_barrier_semaphore()
    for o in range(1, n_t):
        pl.semaphore_signal(barrier, inc=1, device_id=(d, lax.rem(t + o, n_t)), device_id_type=pl.DeviceIdType.MESH)
    for o in range(1, n_dp):
        pl.semaphore_signal(barrier, inc=1, device_id=(lax.rem(d + o, n_dp), t), device_id_type=pl.DeviceIdType.MESH)
    pl.semaphore_wait(barrier, n_t + n_dp - 2)

    def t_copy(stage, src, dst, to, slot):
        return pltpu.make_async_remote_copy(
            src_ref=src, dst_ref=dst, send_sem=t_send.at[stage, to], recv_sem=t_recv.at[stage, slot],
            device_id=(d, to), device_id_type=pl.DeviceIdType.MESH)

    def d_copy(stage, src, dst, to, slot):
        return pltpu.make_async_remote_copy(
            src_ref=src, dst_ref=dst, send_sem=d_send.at[stage, to], recv_sem=d_recv.at[stage, slot],
            device_id=(to, t), device_id_type=pl.DeviceIdType.MESH)

    def t_spread(stage, src, buf):
        for o in (2, 3, 1)[: n_t - 1]:
            t_copy(stage, src, buf.at[t], lax.rem(t + o, n_t), t).start()

    def t_got(stage, buf, p):
        t_copy(stage, buf.at[p], buf.at[p], p, p).wait_recv()

    def d_got(stage, buf, p):
        d_copy(stage, buf, buf, p, p).wait_recv()

    def wslice(p):
        return pl.ds(pl.multiple_of(p * wrows, 16), wrows)

    t_spread(0, x_ref, xg)
    for o in range(1, n_dp):
        d_copy(0, a_ref, ag.at[wslice(d)], lax.rem(d + o, n_dp), d).start()
    t_spread(1, cot_ref, cg)
    for o in range(1, n_dp):
        d_copy(1, b_ref, bg.at[wslice(d)], lax.rem(d + o, n_dp), d).start()
    xg[t] = x_ref[...]
    cg[t] = cot_ref[...]
    ag[wslice(d), :] = a_ref[...]
    bg[wslice(d), :] = b_ref[...]

    segs = seg_ref[...].astype(F32)
    seg_all = jnp.broadcast_to(segs, (rows, span))
    lane_s = lax.broadcasted_iota(jnp.int32, (rows, span), 1)
    row_s = lax.broadcasted_iota(jnp.int32, (rows, span), 0)
    lane_p = lax.broadcasted_iota(jnp.int32, (rows, 128), 1)
    sign = jnp.where(lane_p % 64 < 32, -1.0, 1.0).astype(F32)

    def table_step(j, c):
        place = row_s + j * rows
        column = jnp.sum(jnp.where(lane_s == place, seg_all, 0.0), axis=1, keepdims=True)
        same = seg_all == column
        bias[j] = jnp.where(same, 0.0, -1e30).astype(F32)
        position = jnp.sum(jnp.where(same & (lane_s < place), 1.0, 0.0), axis=1, keepdims=True)
        angle = position * freq_ref[...]
        cosb[j] = jnp.cos(angle)
        sinb[j] = jnp.sin(angle) * sign
        return c

    lax.fori_loop(0, n_t, table_step, 0)

    gain1 = gain1_ref[...]
    gain2 = gain2_ref[...]

    def norm_step(i, c):
        j = lax.rem(t + i, n_t)

        @pl.when(i > 0)
        def _():
            t_got(0, xg, j)

        unit, _ = rms_parts(xg[j].astype(F32))
        n1[j] = (unit * gain1).astype(BF)
        return c

    lax.fori_loop(0, n_t, norm_step, 0)

    for o in range(1, n_dp):
        p = lax.rem(d + o, n_dp)
        d_got(0, ag.at[wslice(p)], p)
    wo[...] = ag[:, qkv_cols:]

    def qkv_step(j, c):
        mixed = dot(n1[j], ag[:, :qkv_cols])
        cosine = cosb[j]
        sine = sinb[j]
        for k in range(2 * n_head // 2):
            chunk = mixed[:, 128 * k:128 * k + 128]
            chunk = chunk * cosine + partner(chunk) * sine
            for half in range(2):
                idx = 2 * k + half
                part = chunk[:, 64 * half:64 * half + 64]
                if idx < n_head:
                    part = part.astype(BF).astype(F32) * 0.125
                qkvh[idx, j] = part.astype(BF)
        for h in range(n_head):
            lo = 2 * head_cols + HD * h
            qkvh[2 * n_head + h, j] = mixed[:, lo:lo + HD].astype(BF)
        return c

    lax.fori_loop(0, n_t, qkv_step, 0)

    def attn_step(i, c):
        h = i // n_t
        j = lax.rem(i, n_t)
        keys = qkvh[n_head + h].reshape(span, HD)
        vals = qkvh[2 * n_head + h].reshape(span, HD)
        s = dot(qkvh[h, j], keys, LAST) + bias[j]
        e = jnp.exp(s - jnp.max(s, axis=-1, keepdims=True))
        p = e * (1.0 / jnp.sum(e, axis=-1, keepdims=True))
        probs[h, j] = p
        hoh[h, j] = dot(p.astype(BF), vals).astype(BF)
        return c

    lax.fori_loop(0, n_head * n_t, attn_step, 0)

    def send_part(stage, part, j, own, snd, rcv):
        @pl.when(j == t)
        def _():
            own[...] = part

        @pl.when(j != t)
        def _():
            snd[j] = part.astype(BF)
            t_copy(stage, snd.at[j], rcv.at[t], j, t).start()

    def order(i):
        return lax.rem(t + (2 + i) * (1 - i // 2) + (3 - i) * (i // 2), n_t)

    def attn_out_step(i, c):
        j = order(i)
        flat = jnp.concatenate([hoh[h, j] for h in range(n_head)], axis=1)
        hof[j] = flat
        send_part(2, dot(flat, wo[...], LAST), j, own1, rs1s, rs1r)
        return c

    lax.fori_loop(0, n_t, attn_out_step, 0)

    def collect(stage, own, rcv):
        total = own[...]
        for o in range(1, n_t):
            p = lax.rem(t + o, n_t)
            t_got(stage, rcv, p)
            total = total + rcv[p].astype(F32)
        return total

    for o in range(1, n_dp):
        p = lax.rem(d + o, n_dp)
        d_got(1, bg.at[wslice(p)], p)
    wg[...] = bg[:, :ff]
    wu[...] = bg[:, ff:2 * ff]
    wd[...] = bg[:, 2 * ff:3 * ff]

    def hidden_step(i, c):
        j = lax.rem(t + i, n_t)

        @pl.when(i > 0)
        def _():
            t_got(1, cg, j)

        ghf[j] = dot(cg[j], wd[...])
        return c

    lax.fori_loop(0, n_t, hidden_step, 0)

    resid_mid = x_ref[...].astype(F32) + collect(2, own1, rs1r)
    mid[...] = resid_mid
    unit, inv2 = rms_parts(resid_mid)
    unit2[...] = unit
    n2g[t] = (unit * gain2).astype(BF)
    t_spread(3, n2g.at[t], n2g)

    def ffn_step(i, c):
        j = lax.rem(t + i, n_t)

        @pl.when(i > 0)
        def _():
            t_got(3, n2g, j)

        gate = dot(n2g[j], wg[...])
        up = dot(n2g[j], wu[...])
        cdf = 0.5 * (1.0 + lax.erf(gate * 0.7071067811865476))
        density = 0.3989422804014327 * jnp.exp(-0.5 * gate * gate)
        val = gate * cdf
        slope = cdf + gate * density
        hidden = (val * up).astype(BF)
        grad_hidden = ghf[j]
        m0 = (grad_hidden * up * slope).astype(BF)
        m1 = (grad_hidden * val).astype(BF)
        hid[j] = hidden
        mix0[j] = m0
        mix1[j] = m1
        send_part(4, dot(m0, wg[...], LAST) + dot(m1, wu[...], LAST), j, own2, rs2s, rs2r)
        send_part(5, dot(hidden, wd[...], LAST), j, own3, rs3s, rs3r)
        return c

    lax.fori_loop(0, n_t, ffn_step, 0)

    grad_two = collect(4, own2, rs2r)
    unit = unit2[...]
    gain_ffn_part = jnp.sum(grad_two * unit, axis=0, keepdims=True)
    grad_mid = cot_ref[...].astype(F32) + norm_back(grad_two, unit, inv2, gain2)
    gmid[...] = grad_mid
    gmg[t] = grad_mid.astype(BF)
    t_spread(6, gmg.at[t], gmg)

    def flat_cols(buf, lo, n):
        return buf[:, :, lo:lo + n].reshape(span, n)

    tile = 256
    hid_all = hid[...].reshape(span, ff)
    mix0_all = mix0[...].reshape(span, ff)
    mix1_all = mix1[...].reshape(span, ff)
    for lo in range(0, width, tile):
        lhs = flat_cols(n2g, lo, tile)
        bgs[lo:lo + tile, :ff] = dot(lhs, mix0_all, FIRST).astype(BF)
        bgs[lo:lo + tile, ff:2 * ff] = dot(lhs, mix1_all, FIRST).astype(BF)
        bgs[lo:lo + tile, 2 * ff:3 * ff] = dot(flat_cols(cg, lo, tile), hid_all, FIRST).astype(BF)
    bgs[:, 3 * ff:] = jnp.zeros((width, bgs.shape[1] - 3 * ff), BF)
    for o in range(1, n_dp):
        p = lax.rem(d + o, n_dp)
        d_copy(2, bgs.at[wslice(p)], bgr.at[d], p, d).start()

    def grad_heads_step(i, c):
        j = lax.rem(t + i, n_t)

        @pl.when(i > 0)
        def _():
            t_got(6, gmg, j)

        gh = dot(gmg[j], wo[...]).astype(BF)
        for h in range(n_head):
            ghh[h, j] = gh[:, HD * h:HD * h + HD]
        return c

    lax.fori_loop(0, n_t, grad_heads_step, 0)

    def attn_back(h, c):
        keys = qkvh[n_head + h].reshape(span, HD)
        vals = qkvh[2 * n_head + h].reshape(span, HD)

        def step(j, c2):
            gh = ghh[h, j]
            row_dot = jnp.sum(gh.astype(F32) * hoh[h, j].astype(F32), axis=-1, keepdims=True)
            ds = (probs[h, j] * (dot(gh, vals, LAST) - row_dot)).astype(BF)
            dsb[j] = ds
            dqkv[h, j] = dot(ds, keys) * 0.125
            return c2

        lax.fori_loop(0, n_t, step, 0)
        dk = dot(dsb[...].reshape(span, span), qkvh[h].reshape(span, HD), FIRST)
        dqkv[n_head + h] = dk.reshape(n_t, rows, HD)
        pb = probs[h].reshape(span, span).astype(BF)
        dv = dot(pb, ghh[h].reshape(span, HD), FIRST)
        dqkv[2 * n_head + h] = dv.reshape(n_t, rows, HD)
        return c

    lax.fori_loop(0, n_head, attn_back, 0)

    def qkv_back_step(i, c):
        j = order(i)
        cosine = cosb[j]
        sine = sinb[j]
        parts = []
        for k in range(n_head):
            chunk = jnp.concatenate([dqkv[2 * k, j], dqkv[2 * k + 1, j]], axis=1)
            parts.append(chunk * cosine - partner(chunk) * sine)
        parts = parts + [dqkv[2 * n_head + h, j] for h in range(n_head)]
        grads = jnp.concatenate(parts, axis=1).astype(BF)
        gq[j] = grads
        send_part(7, dot(grads, ag[:, :qkv_cols], LAST), j, own4, rs4s, rs4r)
        return c

    lax.fori_loop(0, n_t, qkv_back_step, 0)

    gq_all = gq[...].reshape(span, qkv_cols)
    ho_all = hof[...].reshape(span, head_cols)
    for lo in range(0, width, tile):
        ags[lo:lo + tile, :qkv_cols] = dot(flat_cols(n1, lo, tile), gq_all, FIRST).astype(BF)
        ags[lo:lo + tile, qkv_cols:] = dot(flat_cols(gmg, lo, tile), ho_all, FIRST).astype(BF)
    for o in range(1, n_dp):
        p = lax.rem(d + o, n_dp)
        d_copy(3, ags.at[wslice(p)], agr.at[d], p, d).start()

    grad_one = collect(7, own4, rs4r)
    unit1, inv1 = rms_parts(x_ref[...].astype(F32))
    gain_attn_part = jnp.sum(grad_one * unit1, axis=0, keepdims=True)
    gpt[t] = jnp.concatenate([gain_attn_part, gain_ffn_part, jnp.zeros((6, width), F32)], axis=0)
    t_spread(8, gpt.at[t], gpt)
    gin_ref[...] = gmid[...] + norm_back(grad_one, unit1, inv1, gain1)
    out_ref[...] = (mid[...] + collect(5, own3, rs3r)).astype(BF)

    for o in range(1, n_t):
        t_got(8, gpt, lax.rem(t + o, n_t))
    gpd[d] = jnp.sum(gpt[...], axis=0)
    for o in range(1, n_dp):
        d_copy(4, gpd.at[d], gpd.at[d], lax.rem(d + o, n_dp), d).start()

    total = bgs[wslice(d), :].astype(F32)
    for o in range(1, n_dp):
        p = lax.rem(d + o, n_dp)
        d_got(2, bgr.at[p], p)
        total = total + bgr[p].astype(F32)
    gb_ref[...] = total

    total = ags[wslice(d), :].astype(F32)
    for o in range(1, n_dp):
        p = lax.rem(d + o, n_dp)
        d_got(3, agr.at[p], p)
        total = total + agr[p].astype(F32)
    ga_ref[...] = total

    for o in range(1, n_dp):
        p = lax.rem(d + o, n_dp)
        d_got(4, gpd.at[p], p)
    gains_ref[...] = jnp.sum(gpd[...], axis=0)

    for o in range(1, n_t):
        p = lax.rem(t + o, n_t)
        for stage, ref in enumerate((xg, cg, rs1s, n2g, rs2s, rs3s, gmg, rs4s, gpt)):
            t_copy(stage, ref.at[p], ref.at[p], p, p).wait_send()
    for o in range(1, n_dp):
        p = lax.rem(d + o, n_dp)
        for stage, ref in enumerate((a_ref, b_ref, bgr.at[p], agr.at[p], gpd.at[p])):
            d_copy(stage, ref, ref, p, p).wait_send()


def on_device_fused(
    n_dp, n_t,
    inputs, segment_ids, gain_attn, gain_ffn, query_key_value_weight, w_out, w_ffn_in, w_ffn_out, cotangent,
):
    rows, width = inputs.shape
    wrows = w_out.shape[0]
    head_cols = w_out.shape[1]
    ff = w_ffn_out.shape[1]
    if n_t != 4 or wrows % 16 or rows % 128 or head_cols % HD:
        return on_device(
            inputs, segment_ids, gain_attn, gain_ffn, query_key_value_weight, w_out, w_ffn_in, w_ffn_out, cotangent
        )
    n_head = head_cols // HD
    span = n_t * rows
    a_cols = 4 * head_cols
    b_cols = -(-3 * ff // 128) * 128
    block_a = jnp.concatenate([query_key_value_weight.reshape(wrows, -1), w_out], axis=1)
    block_b = jnp.concatenate(
        [w_ffn_in.reshape(wrows, -1), w_ffn_out, jnp.zeros((wrows, b_cols - 3 * ff), BF)], axis=1
    )
    half = np.arange(32, dtype=np.float64)
    freq = np.tile(THETA ** (-2.0 * half / HD), 4).astype(np.float32)[None]
    vmem = pl.BlockSpec(memory_space=pltpu.VMEM)
    act = (n_t, rows, width)

    def v(shape, kind=BF):
        return pltpu.VMEM(shape, kind)

    scratch = [
        v(act), v(act), v((width, a_cols)), v((width, b_cols)), v(act), v(act), v(act),
        v((n_t, rows, 128), F32), v((n_t, rows, 128), F32), v((n_t, rows, span), F32),
        v((3 * n_head, n_t, rows, HD)), v((n_head, n_t, rows, span), F32), v((n_head, n_t, rows, HD)),
        v((n_t, rows, head_cols)), v((width, head_cols)), v((width, ff)), v((width, ff)), v((width, ff)),
        v(act), v(act), v(act), v(act), v(act), v(act), v(act), v(act),
        v((rows, width), F32), v((rows, width), F32), v((rows, width), F32), v((rows, width), F32),
        v((n_t, rows, ff), F32), v((n_t, rows, ff)), v((n_t, rows, ff)), v((n_t, rows, ff)),
        v((rows, width), F32), v((rows, width), F32), v((rows, width), F32),
        v((n_head, n_t, rows, HD)), v((n_t, rows, span)), v((3 * n_head, n_t, rows, HD), F32),
        v((n_t, rows, 3 * head_cols)),
        v((width, a_cols)), v((n_dp, wrows, a_cols)), v((width, b_cols)), v((n_dp, wrows, b_cols)),
        v((n_t, 8, width), F32), v((n_dp, 8, width), F32),
        pltpu.SemaphoreType.DMA((9, n_t)), pltpu.SemaphoreType.DMA((9, n_t)),
        pltpu.SemaphoreType.DMA((5, n_dp)), pltpu.SemaphoreType.DMA((5, n_dp)),
    ]
    result, grad_input, gains, grad_a, grad_b = pl.pallas_call(
        functools.partial(fused_kernel, n_dp, n_t, n_head, ff),
        out_shape=(
            jax.ShapeDtypeStruct((rows, width), BF),
            jax.ShapeDtypeStruct((rows, width), F32),
            jax.ShapeDtypeStruct((8, width), F32),
            jax.ShapeDtypeStruct((wrows, a_cols), F32),
            jax.ShapeDtypeStruct((wrows, b_cols), F32),
        ),
        in_specs=[vmem] * 8,
        out_specs=(vmem,) * 5,
        scratch_shapes=scratch,
        compiler_params=pltpu.CompilerParams(
            collective_id=0, has_side_effects=True, vmem_limit_bytes=60 * 1024 * 1024
        ),
        name="fused_layer",
    )(
        inputs, cotangent, segment_ids, gain_attn[None], gain_ffn[None], jnp.asarray(freq), block_a, block_b,
    )
    return (
        result,
        grad_input,
        gains[0],
        gains[1],
        grad_a[:, : 3 * head_cols].reshape(wrows, 3, head_cols),
        grad_a[:, 3 * head_cols:],
        grad_b[:, : 2 * ff].reshape(wrows, 2, ff),
        grad_b[:, 2 * ff:3 * ff],
    )


def solution(mesh):
    return jax.shard_map(
        functools.partial(on_device_fused, mesh.shape["dp"], mesh.shape["tensor"]),
        mesh=mesh,
        in_specs=(
            P(("dp", "tensor"), None),
            P("dp", None),
            P(),
            P(),
            P("dp", None, "tensor"),
            P("dp", "tensor"),
            P("dp", None, "tensor"),
            P("dp", "tensor"),
            P(("dp", "tensor"), None),
        ),
        out_specs=(
            P(("dp", "tensor"), None),
            P(("dp", "tensor"), None),
            P(),
            P(),
            P("dp", None, "tensor"),
            P("dp", "tensor"),
            P("dp", None, "tensor"),
            P("dp", "tensor"),
        ),
        check_vma=False,
    )
```

```python
import functools

import jax
import jax.numpy as jnp
import numpy as np
from jax import lax
from jax.experimental import pallas as pl
from jax.experimental.pallas import tpu as pltpu
from jax.sharding import PartitionSpec as P

HD = 64


EPS = 1e-05
THETA = 160000.0


def normalize(row_data):
    centre = row_data - jnp.mean(row_data, axis=-1, keepdims=True)
    inverse = lax.rsqrt(jnp.mean(centre * centre, axis=-1, keepdims=True) + EPS)
    return (centre * inverse, inverse)


def norm_back(grad_normed, unit_rows, inverse, gain_row):
    grad_unit = grad_normed * gain_row
    mean_grad = jnp.mean(grad_unit, axis=-1, keepdims=True)
    mean_dot = jnp.mean(grad_unit * unit_rows, axis=-1, keepdims=True)
    return inverse * (grad_unit - mean_grad - unit_rows * mean_dot)


def gelu_parts(values_in):
    normal_cdf = 0.5 * (1.0 + jax.scipy.special.erf(values_in * 0.7071067811865476))
    density = 0.3989422804014327 * jnp.exp(-0.5 * values_in * values_in)
    return (values_in * normal_cdf, normal_cdf + values_in * density)


def rotary_tables(segments, head_size):
    token_count = segments.shape[0]
    places = jnp.arange(token_count, dtype=jnp.int32)
    previous = jnp.concatenate([jnp.full((1,), -1, jnp.int32), segments[:-1]])
    starts = lax.cummax(jnp.where(segments != previous, places, 0), axis=0)
    position = (places - starts).astype(jnp.float32)
    half_size = head_size // 2
    exponent = -(2.0 * jnp.arange(half_size, dtype=jnp.float32)) / head_size
    frequency = jnp.power(jnp.float32(THETA), exponent)
    angles = position[:, None] * frequency[None, :]
    return (jnp.cos(angles), jnp.sin(angles))


def rotate(vectors, cosine, sine):
    half_size = vectors.shape[-1] // 2
    first_half = vectors[..., :half_size]
    second_half = vectors[..., half_size:]
    cos_part = cosine[:, None, :]
    sin_part = sine[:, None, :]
    return jnp.concatenate(
        [
            first_half * cos_part - second_half * sin_part,
            second_half * cos_part + first_half * sin_part,
        ],
        axis=-1,
    )


def block_scores(q_block, keyset, seg_block, segments, scale):
    scores = jnp.einsum("qhe,khe->hqk", q_block, keyset, preferred_element_type=jnp.float32) * scale
    same_seq = seg_block[:, None] == segments[None, :]
    return jnp.where(same_seq[None], scores, jnp.float32(-1e30))


def attention_forward(query, keyset, valueset, segments):
    scale = query.shape[-1] ** (-0.5)
    scores = block_scores(query, keyset, segments, segments, scale)
    top_score = jnp.max(scores, axis=-1, keepdims=True)
    log_total = top_score + jnp.log(jnp.sum(jnp.exp(scores - top_score), axis=-1, keepdims=True))
    probs = jnp.exp(scores - log_total).astype(jnp.bfloat16)
    out_block = jnp.einsum("hqk,khe->qhe", probs, valueset, preferred_element_type=jnp.float32)
    out_list = out_block.astype(jnp.bfloat16)
    return (out_list, log_total)


def attention_backward(query, keyset, valueset, segments, heads_out, log_totals, grad_heads):
    scale = query.shape[-1] ** (-0.5)
    scores = block_scores(query, keyset, segments, segments, scale)
    probs_f = jnp.exp(scores - log_totals)
    probs = probs_f.astype(jnp.bfloat16)
    grad_values = jnp.einsum("hqk,qhe->khe", probs, grad_heads, preferred_element_type=jnp.float32)
    grad_probs = jnp.einsum(
        "qhe,khe->hqk", grad_heads, valueset, preferred_element_type=jnp.float32
    )
    row_dot = jnp.sum(grad_heads.astype(jnp.float32) * heads_out.astype(jnp.float32), axis=-1).T[
        :, :, None
    ]
    grad_scores = (probs_f * (grad_probs - row_dot)).astype(jnp.bfloat16)
    query_list = (
        jnp.einsum("hqk,khe->qhe", grad_scores, keyset, preferred_element_type=jnp.float32) * scale
    )
    grad_keys = (
        jnp.einsum("hqk,qhe->khe", grad_scores, query, preferred_element_type=jnp.float32) * scale
    )
    return (query_list, grad_keys, grad_values)


def spread_rows(row_data):
    return lax.all_gather(row_data, "tensor", axis=0, tiled=True)


def merge_rows(partial_value):
    return lax.psum_scatter(partial_value, "tensor", scatter_dimension=0, tiled=True)


def spread_grads(row_data):
    return lax.all_gather(row_data, "tensor", axis=0, tiled=True)


def merge_grads(partial_value):
    return lax.psum_scatter(partial_value, "tensor", scatter_dimension=0, tiled=True)


def on_device(
    inputs,
    segment_ids,
    gain_attn,
    gain_ffn,
    query_key_value_weight,
    w_out,
    w_ffn_in,
    w_ffn_out,
    cotangent,
):
    query_key_value_full, full_out, full_in, full_down = (
        lax.all_gather(query_key_value_weight, "dp", axis=0, tiled=True),
        lax.all_gather(w_out, "dp", axis=0, tiled=True),
        lax.all_gather(w_ffn_in, "dp", axis=0, tiled=True),
        lax.all_gather(w_ffn_out, "dp", axis=0, tiled=True),
    )
    seg_row = segment_ids[0]
    token_count = seg_row.shape[0]
    contract_last = (((1,), (1,)), ((), ()))
    contract_first = (((0,), (0,)), ((), ()))
    resid_in = inputs.astype(jnp.float32)
    unit_one, inv_one = normalize(resid_in)
    first_normed_rows = spread_rows((unit_one * gain_attn).astype(jnp.bfloat16))
    attention_mixed = jnp.einsum(
        "jk,knr->jnr", first_normed_rows, query_key_value_full, preferred_element_type=jnp.float32
    )
    cosine, sine = rotary_tables(seg_row, HD)
    query = rotate(attention_mixed[:, 0].reshape(token_count, -1, HD), cosine, sine).astype(
        jnp.bfloat16
    )
    keyset = rotate(attention_mixed[:, 1].reshape(token_count, -1, HD), cosine, sine).astype(
        jnp.bfloat16
    )
    valueset = attention_mixed[:, 2].reshape(token_count, -1, HD).astype(jnp.bfloat16)
    heads_out, log_totals = attention_forward(query, keyset, valueset, seg_row)
    flat_out = heads_out.reshape(token_count, -1)
    attn_part = lax.dot_general(
        flat_out, full_out, contract_last, preferred_element_type=jnp.float32
    )
    resid_mid = resid_in + merge_rows(attn_part)
    unit_two, inv_two = normalize(resid_mid)
    normed_two = spread_rows((unit_two * gain_ffn).astype(jnp.bfloat16))
    gate_up = jnp.einsum("td,dsf->tsf", normed_two, full_in, preferred_element_type=jnp.float32)
    gelu_val, gelu_slope = gelu_parts(gate_up[:, 0])
    hidden = (gelu_val * gate_up[:, 1]).astype(jnp.bfloat16)
    ffn_part = lax.dot_general(hidden, full_down, contract_last, preferred_element_type=jnp.float32)
    result = (resid_mid + merge_rows(ffn_part)).astype(jnp.bfloat16)
    query_key_value_back, back_out, back_in, back_down = (
        query_key_value_full,
        full_out,
        full_in,
        full_down,
    )
    grad_top = spread_grads(cotangent)
    down_grad = lax.dot_general(
        grad_top, hidden, contract_first, preferred_element_type=jnp.float32
    )
    grad_hidden = jnp.dot(grad_top, back_down, preferred_element_type=jnp.float32)
    grad_mix = jnp.stack(
        [grad_hidden * gate_up[:, 1] * gelu_slope, grad_hidden * gelu_val], axis=1
    ).astype(jnp.bfloat16)
    in_grad = jnp.einsum("td,tsf->dsf", normed_two, grad_mix, preferred_element_type=jnp.float32)
    grad_two = merge_grads(
        jnp.einsum("tsf,dsf->td", grad_mix, back_in, preferred_element_type=jnp.float32)
    )
    gain_ffn_part = jnp.sum(grad_two * unit_two, axis=0)
    grad_mid = cotangent.astype(jnp.float32) + norm_back(grad_two, unit_two, inv_two, gain_ffn)
    grad_mid_full = spread_grads(grad_mid.astype(jnp.bfloat16))
    out_grad = lax.dot_general(
        grad_mid_full, flat_out, contract_first, preferred_element_type=jnp.float32
    )
    grad_heads = jnp.dot(grad_mid_full, back_out, preferred_element_type=jnp.float32).astype(
        jnp.bfloat16
    )
    grad_heads = grad_heads.reshape(token_count, -1, HD)
    grad_query, grad_keys, grad_values = attention_backward(
        query, keyset, valueset, seg_row, heads_out, log_totals, grad_heads
    )
    grad_query = rotate(grad_query, cosine, -sine)
    grad_keys = rotate(grad_keys, cosine, -sine)
    query_key_value_gradient = jnp.stack(
        [
            grad_query.reshape(token_count, -1),
            grad_keys.reshape(token_count, -1),
            grad_values.reshape(token_count, -1),
        ],
        axis=1,
    ).astype(jnp.bfloat16)
    gradient_query_key_value = jnp.einsum(
        "hz,hjx->zjx",
        first_normed_rows,
        query_key_value_gradient,
        preferred_element_type=jnp.float32,
    )
    first_norm_gradient = merge_grads(
        jnp.einsum(
            "bwi,uwi->bu",
            query_key_value_gradient,
            query_key_value_back,
            preferred_element_type=jnp.float32,
        )
    )
    gain_attn_part = jnp.sum(first_norm_gradient * unit_one, axis=0)
    grad_input = grad_mid + norm_back(first_norm_gradient, unit_one, inv_one, gain_attn)
    gain_attn_grad, gain_ffn_grad = lax.psum((gain_attn_part, gain_ffn_part), ("dp", "tensor"))
    qkv_share, out_share, in_share, down_share = (
        lax.psum_scatter(gradient_query_key_value, "dp", scatter_dimension=0, tiled=True),
        lax.psum_scatter(out_grad, "dp", scatter_dimension=0, tiled=True),
        lax.psum_scatter(in_grad, "dp", scatter_dimension=0, tiled=True),
        lax.psum_scatter(down_grad, "dp", scatter_dimension=0, tiled=True),
    )
    return (
        result,
        grad_input,
        gain_attn_grad,
        gain_ffn_grad,
        qkv_share,
        out_share,
        in_share,
        down_share,
    )


BF = jnp.bfloat16
F32 = jnp.float32
LAST = (((1,), (1,)), ((), ()))
FIRST = (((0,), (0,)), ((), ()))
PLAIN = (((1,), (0,)), ((), ()))


def dot(a, b, dims=PLAIN):
    return lax.dot_general(a, b, dims, preferred_element_type=F32)


def partner(chunk):
    lane = lax.broadcasted_iota(jnp.int32, chunk.shape, 1)
    return jnp.where(lane % 64 < 32, pltpu.roll(chunk, 96, 1), pltpu.roll(chunk, 32, 1))


def rms_parts(rows):
    centre = rows - jnp.mean(rows, axis=-1, keepdims=True)
    inverse = lax.rsqrt(jnp.mean(centre * centre, axis=-1, keepdims=True) + EPS)
    return centre * inverse, inverse


def fused_kernel(
    n_dp, n_t, n_head, ff,
    x_ref, cot_ref, seg_ref, gain1_ref, gain2_ref, freq_ref, a_ref, b_ref,
    out_ref, gin_ref, gains_ref, ga_ref, gb_ref,
    xg, cg, ag, bg, n1, n2g, gmg, cosb, sinb, bias, qkvh, probs, hoh, hof, wo, wg, wu, wd,
    rs1s, rs1r, rs2s, rs2r, rs3s, rs3r, rs4s, rs4r, own1, own2, own3, own4,
    ghf, hid, mix0, mix1, unit2, mid, gmid, ghh, dsb, dqkv, gq, ags, axr, azs, azr, bgs, bxr, bzs, bzr, gpt, gpd,
    t_send, t_recv, d_send, d_recv,
):
    d = lax.axis_index("dp")
    t = lax.axis_index("tensor")
    rows, width = x_ref.shape
    wrows = a_ref.shape[0]
    head_cols = n_head * HD
    qkv_cols = 3 * head_cols
    span = n_t * rows

    barrier = pltpu.get_barrier_semaphore()
    for o in range(1, n_t):
        pl.semaphore_signal(barrier, inc=1, device_id=(d, lax.rem(t + o, n_t)), device_id_type=pl.DeviceIdType.MESH)
    for o in range(1, n_dp):
        pl.semaphore_signal(barrier, inc=1, device_id=(lax.rem(d + o, n_dp), t), device_id_type=pl.DeviceIdType.MESH)
    pl.semaphore_wait(barrier, n_t + n_dp - 2)

    def t_copy(stage, src, dst, to, slot):
        return pltpu.make_async_remote_copy(
            src_ref=src, dst_ref=dst, send_sem=t_send.at[stage, to], recv_sem=t_recv.at[stage, slot],
            device_id=(d, to), device_id_type=pl.DeviceIdType.MESH)

    xx = lax.rem(d, 2)
    zz = d // 2
    n_z = n_dp // 2
    across = d + 1 - 2 * xx
    z_peers = [lax.rem(zz + o, n_z) for o in range(1, n_z)]

    def d_copy(stage, src, dst, to, slot, lane=None, at=None):
        send = d_send.at[stage if lane is None else lane, to if at is None else at]
        return pltpu.make_async_remote_copy(
            src_ref=src, dst_ref=dst, send_sem=send, recv_sem=d_recv.at[stage, slot],
            device_id=(to, t), device_id_type=pl.DeviceIdType.MESH)

    def t_spread(stage, src, buf):
        for o in (2, 3, 1)[: n_t - 1]:
            t_copy(stage, src, buf.at[t], lax.rem(t + o, n_t), t).start()

    def t_got(stage, buf, p):
        t_copy(stage, buf.at[p], buf.at[p], p, p).wait_recv()

    def d_got(stage, buf, p):
        d_copy(stage, buf, buf, p, p).wait_recv()

    def wslice(p):
        return pl.ds(pl.multiple_of(p * wrows, 16), wrows)

    t_spread(0, x_ref, xg)
    for z in z_peers:
        d_copy(0, a_ref, ag.at[wslice(d)], 2 * z + xx, d).start()
    d_copy(0, a_ref, ag.at[wslice(d)], across, d).start()
    t_spread(1, cot_ref, cg)
    for z in z_peers:
        d_copy(1, b_ref, bg.at[wslice(d)], 2 * z + xx, d).start()
    xg[t] = x_ref[...]
    cg[t] = cot_ref[...]
    ag[wslice(d), :] = a_ref[...]
    bg[wslice(d), :] = b_ref[...]

    segs = seg_ref[...].astype(F32)
    seg_all = jnp.broadcast_to(segs, (rows, span))
    lane_s = lax.broadcasted_iota(jnp.int32, (rows, span), 1)
    row_s = lax.broadcasted_iota(jnp.int32, (rows, span), 0)
    lane_p = lax.broadcasted_iota(jnp.int32, (rows, 128), 1)
    sign = jnp.where(lane_p % 64 < 32, -1.0, 1.0).astype(F32)

    def table_step(j, c):
        place = row_s + j * rows
        column = jnp.sum(jnp.where(lane_s == place, seg_all, 0.0), axis=1, keepdims=True)
        same = seg_all == column
        bias[j] = jnp.where(same, 0.0, -1e30).astype(F32)
        position = jnp.sum(jnp.where(same & (lane_s < place), 1.0, 0.0), axis=1, keepdims=True)
        angle = position * freq_ref[...]
        cosb[j] = jnp.cos(angle)
        sinb[j] = jnp.sin(angle) * sign
        return c

    lax.fori_loop(0, n_t, table_step, 0)

    gain1 = gain1_ref[...]
    gain2 = gain2_ref[...]

    def norm_step(i, c):
        j = lax.rem(t + i, n_t)

        @pl.when(i > 0)
        def _():
            t_got(0, xg, j)

        unit, _ = rms_parts(xg[j].astype(F32))
        n1[j] = (unit * gain1).astype(BF)
        return c

    lax.fori_loop(0, n_t, norm_step, 0)

    def pass_on(stage, buf, z):
        p = 2 * z + xx
        d_got(stage, buf.at[wslice(p)], p)
        d_copy(stage, buf.at[wslice(p)], buf.at[wslice(p)], across, p, 5 + stage, p).start()

    def from_across(stage, buf):
        for z in range(n_z):
            p = 2 * z + 1 - xx
            d_got(stage, buf.at[wslice(p)], p)

    for z in z_peers:
        pass_on(0, ag, z)
    d_copy(1, b_ref, bg.at[wslice(d)], across, d).start()
    from_across(0, ag)
    wo[...] = ag[:, qkv_cols:]

    def qkv_step(j, c):
        mixed = dot(n1[j], ag[:, :qkv_cols])
        cosine = cosb[j]
        sine = sinb[j]
        for k in range(2 * n_head // 2):
            chunk = mixed[:, 128 * k:128 * k + 128]
            chunk = chunk * cosine + partner(chunk) * sine
            for half in range(2):
                idx = 2 * k + half
                part = chunk[:, 64 * half:64 * half + 64]
                if idx < n_head:
                    part = part.astype(BF).astype(F32) * 0.125
                qkvh[idx, j] = part.astype(BF)
        for h in range(n_head):
            lo = 2 * head_cols + HD * h
            qkvh[2 * n_head + h, j] = mixed[:, lo:lo + HD].astype(BF)
        return c

    lax.fori_loop(0, n_t, qkv_step, 0)

    def attn_step(h, j, c):
        keys = qkvh[n_head + h].reshape(span, HD)
        vals = qkvh[2 * n_head + h].reshape(span, HD)
        s = dot(qkvh[h, j], keys, LAST) + bias[j]
        e = jnp.exp(s - jnp.max(s, axis=-1, keepdims=True))
        p = e * (1.0 / jnp.sum(e, axis=-1, keepdims=True))
        probs[h, j] = p
        hoh[h, j] = dot(p.astype(BF), vals).astype(BF)
        return c

    passed = 0
    for h in range(n_head):
        lax.fori_loop(0, n_t, functools.partial(attn_step, h), 0)
        until = n_z - 1 if h == n_head - 1 else min(passed + 1, n_z - 1)
        for z in z_peers[passed:until]:
            pass_on(1, bg, z)
        passed = until

    def send_part(stage, part, j, own, snd, rcv):
        @pl.when(j == t)
        def _():
            own[...] = part

        @pl.when(j != t)
        def _():
            snd[j] = part.astype(BF)
            t_copy(stage, snd.at[j], rcv.at[t], j, t).start()

    def order(i):
        return lax.rem(t + (2 + i) * (1 - i // 2) + (3 - i) * (i // 2), n_t)

    def attn_out_step(i, c):
        j = order(i)
        flat = jnp.concatenate([hoh[h, j] for h in range(n_head)], axis=1)
        hof[j] = flat
        send_part(2, dot(flat, wo[...], LAST), j, own1, rs1s, rs1r)
        return c

    lax.fori_loop(0, n_t, attn_out_step, 0)

    def collect(stage, own, rcv):
        total = own[...]
        for o in range(1, n_t):
            p = lax.rem(t + o, n_t)
            t_got(stage, rcv, p)
            total = total + rcv[p].astype(F32)
        return total

    from_across(1, bg)
    wg[...] = bg[:, :ff]
    wu[...] = bg[:, ff:2 * ff]
    wd[...] = bg[:, 2 * ff:3 * ff]

    def hidden_step(i, c):
        j = lax.rem(t + i, n_t)

        @pl.when(i > 0)
        def _():
            t_got(1, cg, j)

        ghf[j] = dot(cg[j], wd[...])
        return c

    lax.fori_loop(0, n_t, hidden_step, 0)

    resid_mid = x_ref[...].astype(F32) + collect(2, own1, rs1r)
    mid[...] = resid_mid
    unit, inv2 = rms_parts(resid_mid)
    unit2[...] = unit
    n2g[t] = (unit * gain2).astype(BF)
    t_spread(3, n2g.at[t], n2g)

    def ffn_step(i, c):
        j = lax.rem(t + i, n_t)

        @pl.when(i > 0)
        def _():
            t_got(3, n2g, j)

        gate = dot(n2g[j], wg[...])
        up = dot(n2g[j], wu[...])
        cdf = 0.5 * (1.0 + lax.erf(gate * 0.7071067811865476))
        density = 0.3989422804014327 * jnp.exp(-0.5 * gate * gate)
        val = gate * cdf
        slope = cdf + gate * density
        hidden = (val * up).astype(BF)
        grad_hidden = ghf[j]
        m0 = (grad_hidden * up * slope).astype(BF)
        m1 = (grad_hidden * val).astype(BF)
        hid[j] = hidden
        mix0[j] = m0
        mix1[j] = m1
        send_part(4, dot(m0, wg[...], LAST) + dot(m1, wu[...], LAST), j, own2, rs2s, rs2r)
        send_part(5, dot(hidden, wd[...], LAST), j, own3, rs3s, rs3r)
        return c

    lax.fori_loop(0, n_t, ffn_step, 0)

    grad_two = collect(4, own2, rs2r)
    unit = unit2[...]
    gain_ffn_part = jnp.sum(grad_two * unit, axis=0, keepdims=True)
    grad_mid = cot_ref[...].astype(F32) + norm_back(grad_two, unit, inv2, gain2)
    gmid[...] = grad_mid
    gmg[t] = grad_mid.astype(BF)
    t_spread(6, gmg.at[t], gmg)

    def flat_cols(buf, lo, n):
        return buf[:, :, lo:lo + n].reshape(span, n)

    tile = 256
    hid_all = hid[...].reshape(span, ff)
    mix0_all = mix0[...].reshape(span, ff)
    mix1_all = mix1[...].reshape(span, ff)
    for lo in range(0, width, tile):
        lhs = flat_cols(n2g, lo, tile)
        bgs[lo:lo + tile, :ff] = dot(lhs, mix0_all, FIRST).astype(BF)
        bgs[lo:lo + tile, ff:2 * ff] = dot(lhs, mix1_all, FIRST).astype(BF)
        bgs[lo:lo + tile, 2 * ff:3 * ff] = dot(flat_cols(cg, lo, tile), hid_all, FIRST).astype(BF)
    bgs[:, 3 * ff:] = jnp.zeros((width, bgs.shape[1] - 3 * ff), BF)

    def reduce_across(stage, snd, rcv):
        for z in range(n_z):
            d_copy(stage, snd.at[wslice(2 * z + 1 - xx)], rcv.at[z], across, z, stage, z).start()

    def reduce_along(stage, snd, rcv, sums, got):
        for z in z_peers:
            d_got(stage, rcv.at[z], z)
            sums[z] = (snd[wslice(2 * z + xx), :].astype(F32) + rcv[z].astype(F32)).astype(BF)
            d_copy(stage + 5, sums.at[z], got.at[zz], 2 * z + xx, zz, stage + 5, z).start()

    def reduce_end(stage, snd, rcv, got):
        d_got(stage, rcv.at[zz], zz)
        total = snd[wslice(d), :].astype(F32) + rcv[zz].astype(F32)
        for z in z_peers:
            d_got(stage + 5, got.at[z], z)
            total = total + got[z].astype(F32)
        return total

    reduce_across(2, bgs, bxr)

    def grad_heads_step(i, c):
        j = lax.rem(t + i, n_t)

        @pl.when(i > 0)
        def _():
            t_got(6, gmg, j)

        gh = dot(gmg[j], wo[...]).astype(BF)
        for h in range(n_head):
            ghh[h, j] = gh[:, HD * h:HD * h + HD]
        return c

    lax.fori_loop(0, n_t, grad_heads_step, 0)

    def attn_back(h, c):
        keys = qkvh[n_head + h].reshape(span, HD)
        vals = qkvh[2 * n_head + h].reshape(span, HD)

        def step(j, c2):
            gh = ghh[h, j]
            row_dot = jnp.sum(gh.astype(F32) * hoh[h, j].astype(F32), axis=-1, keepdims=True)
            ds = (probs[h, j] * (dot(gh, vals, LAST) - row_dot)).astype(BF)
            dsb[j] = ds
            dqkv[h, j] = dot(ds, keys) * 0.125
            return c2

        lax.fori_loop(0, n_t, step, 0)
        dk = dot(dsb[...].reshape(span, span), qkvh[h].reshape(span, HD), FIRST)
        dqkv[n_head + h] = dk.reshape(n_t, rows, HD)
        pb = probs[h].reshape(span, span).astype(BF)
        dv = dot(pb, ghh[h].reshape(span, HD), FIRST)
        dqkv[2 * n_head + h] = dv.reshape(n_t, rows, HD)
        return c

    lax.fori_loop(0, n_head, attn_back, 0)

    reduce_along(2, bgs, bxr, bzs, bzr)

    def unrotate_step(j, c):
        cosine = cosb[j]
        sine = sinb[j]
        parts = []
        for k in range(n_head):
            chunk = jnp.concatenate([dqkv[2 * k, j], dqkv[2 * k + 1, j]], axis=1)
            parts.append(chunk * cosine - partner(chunk) * sine)
        parts = parts + [dqkv[2 * n_head + h, j] for h in range(n_head)]
        gq[j] = jnp.concatenate(parts, axis=1).astype(BF)
        return c

    lax.fori_loop(0, n_t, unrotate_step, 0)

    gq_all = gq[...].reshape(span, qkv_cols)
    ho_all = hof[...].reshape(span, head_cols)
    for lo in range(0, width, tile):
        ags[lo:lo + tile, :qkv_cols] = dot(flat_cols(n1, lo, tile), gq_all, FIRST).astype(BF)
        ags[lo:lo + tile, qkv_cols:] = dot(flat_cols(gmg, lo, tile), ho_all, FIRST).astype(BF)
    reduce_across(3, ags, axr)

    def qkv_back_step(i, c):
        j = order(i)
        send_part(7, dot(gq[j], ag[:, :qkv_cols], LAST), j, own4, rs4s, rs4r)
        return c

    lax.fori_loop(0, n_t, qkv_back_step, 0)
    reduce_along(3, ags, axr, azs, azr)

    grad_one = collect(7, own4, rs4r)
    unit1, inv1 = rms_parts(x_ref[...].astype(F32))
    gain_attn_part = jnp.sum(grad_one * unit1, axis=0, keepdims=True)
    gpt[t] = jnp.concatenate([gain_attn_part, gain_ffn_part, jnp.zeros((6, width), F32)], axis=0)
    t_spread(8, gpt.at[t], gpt)
    gin_ref[...] = gmid[...] + norm_back(grad_one, unit1, inv1, gain1)
    out_ref[...] = (mid[...] + collect(5, own3, rs3r)).astype(BF)

    for o in range(1, n_t):
        t_got(8, gpt, lax.rem(t + o, n_t))
    gpd[d] = jnp.sum(gpt[...], axis=0)
    for o in range(1, n_dp):
        d_copy(4, gpd.at[d], gpd.at[d], lax.rem(d + o, n_dp), d).start()

    gb_ref[...] = reduce_end(2, bgs, bxr, bzr)
    ga_ref[...] = reduce_end(3, ags, axr, azr)

    for o in range(1, n_dp):
        p = lax.rem(d + o, n_dp)
        d_got(4, gpd.at[p], p)
    gains_ref[...] = jnp.sum(gpd[...], axis=0)

    for o in range(1, n_t):
        p = lax.rem(t + o, n_t)
        for stage, ref in enumerate((xg, cg, rs1s, n2g, rs2s, rs3s, gmg, rs4s, gpt)):
            t_copy(stage, ref.at[p], ref.at[p], p, p).wait_send()

    def d_sent(lane, ref, at):
        d_copy(0, ref, ref, across, d, lane, at).wait_send()

    for o in range(1, n_dp):
        d_sent(4, gpd.at[d], lax.rem(d + o, n_dp))
    for lane, own, part, sums in ((0, a_ref, axr, azs), (1, b_ref, bxr, bzs)):
        d_sent(lane, own, across)
        for z in z_peers:
            d_sent(lane, own, 2 * z + xx)
            d_sent(lane + 5, own, 2 * z + xx)
            d_sent(8 - lane, sums.at[z], z)
        for z in range(n_z):
            d_sent(3 - lane, part.at[z], z)


def on_device_fused(
    n_dp, n_t,
    inputs, segment_ids, gain_attn, gain_ffn, query_key_value_weight, w_out, w_ffn_in, w_ffn_out, cotangent,
):
    rows, width = inputs.shape
    wrows = w_out.shape[0]
    head_cols = w_out.shape[1]
    ff = w_ffn_out.shape[1]
    if n_t != 4 or n_dp % 2 or wrows % 16 or rows % 128 or head_cols % HD:
        return on_device(
            inputs, segment_ids, gain_attn, gain_ffn, query_key_value_weight, w_out, w_ffn_in, w_ffn_out, cotangent
        )
    n_head = head_cols // HD
    span = n_t * rows
    a_cols = 4 * head_cols
    b_cols = -(-3 * ff // 128) * 128
    block_a = jnp.concatenate([query_key_value_weight.reshape(wrows, -1), w_out], axis=1)
    block_b = jnp.concatenate(
        [w_ffn_in.reshape(wrows, -1), w_ffn_out, jnp.zeros((wrows, b_cols - 3 * ff), BF)], axis=1
    )
    half = np.arange(32, dtype=np.float64)
    freq = np.tile(THETA ** (-2.0 * half / HD), 4).astype(np.float32)[None]
    vmem = pl.BlockSpec(memory_space=pltpu.VMEM)
    act = (n_t, rows, width)

    part_a = (n_dp // 2, wrows, a_cols)
    part_b = (n_dp // 2, wrows, b_cols)

    def v(shape, kind=BF):
        return pltpu.VMEM(shape, kind)

    scratch = [
        v(act), v(act), v((width, a_cols)), v((width, b_cols)), v(act), v(act), v(act),
        v((n_t, rows, 128), F32), v((n_t, rows, 128), F32), v((n_t, rows, span), F32),
        v((3 * n_head, n_t, rows, HD)), v((n_head, n_t, rows, span), F32), v((n_head, n_t, rows, HD)),
        v((n_t, rows, head_cols)), v((width, head_cols)), v((width, ff)), v((width, ff)), v((width, ff)),
        v(act), v(act), v(act), v(act), v(act), v(act), v(act), v(act),
        v((rows, width), F32), v((rows, width), F32), v((rows, width), F32), v((rows, width), F32),
        v((n_t, rows, ff), F32), v((n_t, rows, ff)), v((n_t, rows, ff)), v((n_t, rows, ff)),
        v((rows, width), F32), v((rows, width), F32), v((rows, width), F32),
        v((n_head, n_t, rows, HD)), v((n_t, rows, span)), v((3 * n_head, n_t, rows, HD), F32),
        v((n_t, rows, 3 * head_cols)),
        v((width, a_cols)), v(part_a), v(part_a), v(part_a), v((width, b_cols)), v(part_b), v(part_b), v(part_b),
        v((n_t, 8, width), F32), v((n_dp, 8, width), F32),
        pltpu.SemaphoreType.DMA((9, n_t)), pltpu.SemaphoreType.DMA((9, n_t)),
        pltpu.SemaphoreType.DMA((9, n_dp)), pltpu.SemaphoreType.DMA((9, n_dp)),
    ]
    result, grad_input, gains, grad_a, grad_b = pl.pallas_call(
        functools.partial(fused_kernel, n_dp, n_t, n_head, ff),
        out_shape=(
            jax.ShapeDtypeStruct((rows, width), BF),
            jax.ShapeDtypeStruct((rows, width), F32),
            jax.ShapeDtypeStruct((8, width), F32),
            jax.ShapeDtypeStruct((wrows, a_cols), F32),
            jax.ShapeDtypeStruct((wrows, b_cols), F32),
        ),
        in_specs=[vmem] * 8,
        out_specs=(vmem,) * 5,
        scratch_shapes=scratch,
        compiler_params=pltpu.CompilerParams(
            collective_id=0, has_side_effects=True, vmem_limit_bytes=60 * 1024 * 1024
        ),
        name="fused_layer",
    )(
        inputs, cotangent, segment_ids, gain_attn[None], gain_ffn[None], jnp.asarray(freq), block_a, block_b,
    )
    return (
        result,
        grad_input,
        gains[0],
        gains[1],
        grad_a[:, : 3 * head_cols].reshape(wrows, 3, head_cols),
        grad_a[:, 3 * head_cols:],
        grad_b[:, : 2 * ff].reshape(wrows, 2, ff),
        grad_b[:, 2 * ff:3 * ff],
    )


def solution(mesh):
    return jax.shard_map(
        functools.partial(on_device_fused, mesh.shape["dp"], mesh.shape["tensor"]),
        mesh=mesh,
        in_specs=(
            P(("dp", "tensor"), None),
            P("dp", None),
            P(),
            P(),
            P("dp", None, "tensor"),
            P("dp", "tensor"),
            P("dp", None, "tensor"),
            P("dp", "tensor"),
            P(("dp", "tensor"), None),
        ),
        out_specs=(
            P(("dp", "tensor"), None),
            P(("dp", "tensor"), None),
            P(),
            P(),
            P("dp", None, "tensor"),
            P("dp", "tensor"),
            P("dp", None, "tensor"),
            P("dp", "tensor"),
        ),
        check_vma=False,
    )
```

```python
import functools

import jax
import jax.numpy as jnp
import numpy as np
from jax import lax
from jax.experimental import pallas as pl
from jax.experimental.pallas import tpu as pltpu
from jax.sharding import PartitionSpec as P

HD = 64


EPS = 1e-05
THETA = 160000.0


def normalize(row_data):
    centre = row_data - jnp.mean(row_data, axis=-1, keepdims=True)
    inverse = lax.rsqrt(jnp.mean(centre * centre, axis=-1, keepdims=True) + EPS)
    return (centre * inverse, inverse)


def norm_back(grad_normed, unit_rows, inverse, gain_row):
    grad_unit = grad_normed * gain_row
    mean_grad = jnp.mean(grad_unit, axis=-1, keepdims=True)
    mean_dot = jnp.mean(grad_unit * unit_rows, axis=-1, keepdims=True)
    return inverse * (grad_unit - mean_grad - unit_rows * mean_dot)


def gelu_parts(values_in):
    normal_cdf = 0.5 * (1.0 + jax.scipy.special.erf(values_in * 0.7071067811865476))
    density = 0.3989422804014327 * jnp.exp(-0.5 * values_in * values_in)
    return (values_in * normal_cdf, normal_cdf + values_in * density)


def rotary_tables(segments, head_size):
    token_count = segments.shape[0]
    places = jnp.arange(token_count, dtype=jnp.int32)
    previous = jnp.concatenate([jnp.full((1,), -1, jnp.int32), segments[:-1]])
    starts = lax.cummax(jnp.where(segments != previous, places, 0), axis=0)
    position = (places - starts).astype(jnp.float32)
    half_size = head_size // 2
    exponent = -(2.0 * jnp.arange(half_size, dtype=jnp.float32)) / head_size
    frequency = jnp.power(jnp.float32(THETA), exponent)
    angles = position[:, None] * frequency[None, :]
    return (jnp.cos(angles), jnp.sin(angles))


def rotate(vectors, cosine, sine):
    half_size = vectors.shape[-1] // 2
    first_half = vectors[..., :half_size]
    second_half = vectors[..., half_size:]
    cos_part = cosine[:, None, :]
    sin_part = sine[:, None, :]
    return jnp.concatenate(
        [
            first_half * cos_part - second_half * sin_part,
            second_half * cos_part + first_half * sin_part,
        ],
        axis=-1,
    )


def block_scores(q_block, keyset, seg_block, segments, scale):
    scores = jnp.einsum("qhe,khe->hqk", q_block, keyset, preferred_element_type=jnp.float32) * scale
    same_seq = seg_block[:, None] == segments[None, :]
    return jnp.where(same_seq[None], scores, jnp.float32(-1e30))


def attention_forward(query, keyset, valueset, segments):
    scale = query.shape[-1] ** (-0.5)
    scores = block_scores(query, keyset, segments, segments, scale)
    top_score = jnp.max(scores, axis=-1, keepdims=True)
    log_total = top_score + jnp.log(jnp.sum(jnp.exp(scores - top_score), axis=-1, keepdims=True))
    probs = jnp.exp(scores - log_total).astype(jnp.bfloat16)
    out_block = jnp.einsum("hqk,khe->qhe", probs, valueset, preferred_element_type=jnp.float32)
    out_list = out_block.astype(jnp.bfloat16)
    return (out_list, log_total)


def attention_backward(query, keyset, valueset, segments, heads_out, log_totals, grad_heads):
    scale = query.shape[-1] ** (-0.5)
    scores = block_scores(query, keyset, segments, segments, scale)
    probs_f = jnp.exp(scores - log_totals)
    probs = probs_f.astype(jnp.bfloat16)
    grad_values = jnp.einsum("hqk,qhe->khe", probs, grad_heads, preferred_element_type=jnp.float32)
    grad_probs = jnp.einsum(
        "qhe,khe->hqk", grad_heads, valueset, preferred_element_type=jnp.float32
    )
    row_dot = jnp.sum(grad_heads.astype(jnp.float32) * heads_out.astype(jnp.float32), axis=-1).T[
        :, :, None
    ]
    grad_scores = (probs_f * (grad_probs - row_dot)).astype(jnp.bfloat16)
    query_list = (
        jnp.einsum("hqk,khe->qhe", grad_scores, keyset, preferred_element_type=jnp.float32) * scale
    )
    grad_keys = (
        jnp.einsum("hqk,qhe->khe", grad_scores, query, preferred_element_type=jnp.float32) * scale
    )
    return (query_list, grad_keys, grad_values)


def spread_rows(row_data):
    return lax.all_gather(row_data, "tensor", axis=0, tiled=True)


def merge_rows(partial_value):
    return lax.psum_scatter(partial_value, "tensor", scatter_dimension=0, tiled=True)


def spread_grads(row_data):
    return lax.all_gather(row_data, "tensor", axis=0, tiled=True)


def merge_grads(partial_value):
    return lax.psum_scatter(partial_value, "tensor", scatter_dimension=0, tiled=True)


def on_device(
    inputs,
    segment_ids,
    gain_attn,
    gain_ffn,
    query_key_value_weight,
    w_out,
    w_ffn_in,
    w_ffn_out,
    cotangent,
):
    query_key_value_full, full_out, full_in, full_down = (
        lax.all_gather(query_key_value_weight, "dp", axis=0, tiled=True),
        lax.all_gather(w_out, "dp", axis=0, tiled=True),
        lax.all_gather(w_ffn_in, "dp", axis=0, tiled=True),
        lax.all_gather(w_ffn_out, "dp", axis=0, tiled=True),
    )
    seg_row = segment_ids[0]
    token_count = seg_row.shape[0]
    contract_last = (((1,), (1,)), ((), ()))
    contract_first = (((0,), (0,)), ((), ()))
    resid_in = inputs.astype(jnp.float32)
    unit_one, inv_one = normalize(resid_in)
    first_normed_rows = spread_rows((unit_one * gain_attn).astype(jnp.bfloat16))
    attention_mixed = jnp.einsum(
        "jk,knr->jnr", first_normed_rows, query_key_value_full, preferred_element_type=jnp.float32
    )
    cosine, sine = rotary_tables(seg_row, HD)
    query = rotate(attention_mixed[:, 0].reshape(token_count, -1, HD), cosine, sine).astype(
        jnp.bfloat16
    )
    keyset = rotate(attention_mixed[:, 1].reshape(token_count, -1, HD), cosine, sine).astype(
        jnp.bfloat16
    )
    valueset = attention_mixed[:, 2].reshape(token_count, -1, HD).astype(jnp.bfloat16)
    heads_out, log_totals = attention_forward(query, keyset, valueset, seg_row)
    flat_out = heads_out.reshape(token_count, -1)
    attn_part = lax.dot_general(
        flat_out, full_out, contract_last, preferred_element_type=jnp.float32
    )
    resid_mid = resid_in + merge_rows(attn_part)
    unit_two, inv_two = normalize(resid_mid)
    normed_two = spread_rows((unit_two * gain_ffn).astype(jnp.bfloat16))
    gate_up = jnp.einsum("td,dsf->tsf", normed_two, full_in, preferred_element_type=jnp.float32)
    gelu_val, gelu_slope = gelu_parts(gate_up[:, 0])
    hidden = (gelu_val * gate_up[:, 1]).astype(jnp.bfloat16)
    ffn_part = lax.dot_general(hidden, full_down, contract_last, preferred_element_type=jnp.float32)
    result = (resid_mid + merge_rows(ffn_part)).astype(jnp.bfloat16)
    query_key_value_back, back_out, back_in, back_down = (
        query_key_value_full,
        full_out,
        full_in,
        full_down,
    )
    grad_top = spread_grads(cotangent)
    down_grad = lax.dot_general(
        grad_top, hidden, contract_first, preferred_element_type=jnp.float32
    )
    grad_hidden = jnp.dot(grad_top, back_down, preferred_element_type=jnp.float32)
    grad_mix = jnp.stack(
        [grad_hidden * gate_up[:, 1] * gelu_slope, grad_hidden * gelu_val], axis=1
    ).astype(jnp.bfloat16)
    in_grad = jnp.einsum("td,tsf->dsf", normed_two, grad_mix, preferred_element_type=jnp.float32)
    grad_two = merge_grads(
        jnp.einsum("tsf,dsf->td", grad_mix, back_in, preferred_element_type=jnp.float32)
    )
    gain_ffn_part = jnp.sum(grad_two * unit_two, axis=0)
    grad_mid = cotangent.astype(jnp.float32) + norm_back(grad_two, unit_two, inv_two, gain_ffn)
    grad_mid_full = spread_grads(grad_mid.astype(jnp.bfloat16))
    out_grad = lax.dot_general(
        grad_mid_full, flat_out, contract_first, preferred_element_type=jnp.float32
    )
    grad_heads = jnp.dot(grad_mid_full, back_out, preferred_element_type=jnp.float32).astype(
        jnp.bfloat16
    )
    grad_heads = grad_heads.reshape(token_count, -1, HD)
    grad_query, grad_keys, grad_values = attention_backward(
        query, keyset, valueset, seg_row, heads_out, log_totals, grad_heads
    )
    grad_query = rotate(grad_query, cosine, -sine)
    grad_keys = rotate(grad_keys, cosine, -sine)
    query_key_value_gradient = jnp.stack(
        [
            grad_query.reshape(token_count, -1),
            grad_keys.reshape(token_count, -1),
            grad_values.reshape(token_count, -1),
        ],
        axis=1,
    ).astype(jnp.bfloat16)
    gradient_query_key_value = jnp.einsum(
        "hz,hjx->zjx",
        first_normed_rows,
        query_key_value_gradient,
        preferred_element_type=jnp.float32,
    )
    first_norm_gradient = merge_grads(
        jnp.einsum(
            "bwi,uwi->bu",
            query_key_value_gradient,
            query_key_value_back,
            preferred_element_type=jnp.float32,
        )
    )
    gain_attn_part = jnp.sum(first_norm_gradient * unit_one, axis=0)
    grad_input = grad_mid + norm_back(first_norm_gradient, unit_one, inv_one, gain_attn)
    gain_attn_grad, gain_ffn_grad = lax.psum((gain_attn_part, gain_ffn_part), ("dp", "tensor"))
    qkv_share, out_share, in_share, down_share = (
        lax.psum_scatter(gradient_query_key_value, "dp", scatter_dimension=0, tiled=True),
        lax.psum_scatter(out_grad, "dp", scatter_dimension=0, tiled=True),
        lax.psum_scatter(in_grad, "dp", scatter_dimension=0, tiled=True),
        lax.psum_scatter(down_grad, "dp", scatter_dimension=0, tiled=True),
    )
    return (
        result,
        grad_input,
        gain_attn_grad,
        gain_ffn_grad,
        qkv_share,
        out_share,
        in_share,
        down_share,
    )


BF = jnp.bfloat16
F32 = jnp.float32
LAST = (((1,), (1,)), ((), ()))
FIRST = (((0,), (0,)), ((), ()))
PLAIN = (((1,), (0,)), ((), ()))


def dot(a, b, dims=PLAIN):
    return lax.dot_general(a, b, dims, preferred_element_type=F32)


def partner(chunk):
    lane = lax.broadcasted_iota(jnp.int32, chunk.shape, 1)
    return jnp.where(lane % 64 < 32, pltpu.roll(chunk, 96, 1), pltpu.roll(chunk, 32, 1))


def rms_parts(rows):
    centre = rows - jnp.mean(rows, axis=-1, keepdims=True)
    inverse = lax.rsqrt(jnp.mean(centre * centre, axis=-1, keepdims=True) + EPS)
    return centre * inverse, inverse


def fused_kernel(
    n_dp, n_t, n_head, ff,
    x_ref, cot_ref, seg_ref, gain1_ref, gain2_ref, freq_ref, wqkv_ref, wout_ref, win_ref, wdown_ref,
    out_ref, gin_ref, gain1_out, gain2_out, gqkv_ref, gwo_ref, gin_w_ref, gdown_ref,
    xg, cg, ag, bg, n1, n2g, gmg, cosb, sinb, bias, qkvh, probs, hoh, hof, wo, wg, wu, wd,
    rs1s, rs1r, rs2s, rs2r, rs3s, rs3r, rs4s, rs4r, own1, own2, own3, own4,
    ghf, hid, mix0, mix1, unit2, mid, gmid, ghh, dsb, dqkv, gq, ags, axr, azs, azr, bgs, bxr, bzs, bzr, gpt, gpd, a_ref, b_ref,
    t_send, t_recv, d_send, d_recv,
):
    d = lax.axis_index("dp")
    t = lax.axis_index("tensor")
    rows, width = x_ref.shape
    wrows = wout_ref.shape[0]
    head_cols = n_head * HD
    qkv_cols = 3 * head_cols
    span = n_t * rows

    barrier = pltpu.get_barrier_semaphore()
    for o in range(1, n_t):
        pl.semaphore_signal(barrier, inc=1, device_id=(d, lax.rem(t + o, n_t)), device_id_type=pl.DeviceIdType.MESH)
    for o in range(1, n_dp):
        pl.semaphore_signal(barrier, inc=1, device_id=(lax.rem(d + o, n_dp), t), device_id_type=pl.DeviceIdType.MESH)
    a_ref[...] = jnp.concatenate([wqkv_ref[0], wqkv_ref[1], wqkv_ref[2], wout_ref[...]], axis=1)
    b_pad = jnp.zeros((wrows, b_ref.shape[1] - 3 * ff), BF)
    b_ref[...] = jnp.concatenate([win_ref[0], win_ref[1], wdown_ref[...], b_pad], axis=1)
    pl.semaphore_wait(barrier, n_t + n_dp - 2)

    def t_copy(stage, src, dst, to, slot, at=None):
        return pltpu.make_async_remote_copy(
            src_ref=src, dst_ref=dst, send_sem=t_send.at[stage, to if at is None else at], recv_sem=t_recv.at[stage, slot],
            device_id=(d, to), device_id_type=pl.DeviceIdType.MESH)

    xx = lax.rem(d, 2)
    zz = d // 2
    n_z = n_dp // 2
    across = d + 1 - 2 * xx
    z_peers = [lax.rem(zz + o, n_z) for o in range(1, n_z)]

    def d_copy(stage, src, dst, to, slot, lane=None, at=None):
        send = d_send.at[stage if lane is None else lane, to if at is None else at]
        return pltpu.make_async_remote_copy(
            src_ref=src, dst_ref=dst, send_sem=send, recv_sem=d_recv.at[stage, slot],
            device_id=(to, t), device_id_type=pl.DeviceIdType.MESH)

    over = lax.rem(t + 2, n_t)
    other = t + 1 - 2 * lax.rem(t, 2)

    def t_relay(stage, buf):
        t_got(stage, buf, over)
        far_copy = t_copy(stage, buf.at[over], buf.at[over], other, over, t)
        far_copy.start()

    def t_spread(stage, src, buf):
        for to in (over, other):
            t_copy(stage, src, buf.at[t], to, t).start()

    def t_got(stage, buf, p):
        t_copy(stage, buf.at[p], buf.at[p], p, p).wait_recv()

    def d_got(stage, buf, p):
        d_copy(stage, buf, buf, p, p).wait_recv()

    far = lax.rem(other + 2, n_t)

    def visit(i):
        first = over * (i % 2) + t * (1 - i % 2)
        last = far * (i % 2) + other * (1 - i % 2)
        return first * (1 - i // 2) + last * (i // 2)

    def wslice(p):
        return pl.ds(pl.multiple_of(p * wrows, 16), wrows)

    t_spread(0, x_ref, xg)
    for z in z_peers:
        d_copy(0, a_ref, ag.at[wslice(d)], 2 * z + xx, d).start()
    d_copy(0, a_ref, ag.at[wslice(d)], across, d).start()
    t_spread(1, cot_ref, cg)
    xg[t] = x_ref[...]
    cg[t] = cot_ref[...]
    ag[wslice(d), :] = a_ref[...]
    bg[wslice(d), :] = b_ref[...]

    segs = seg_ref[...].astype(F32)
    seg_all = jnp.broadcast_to(segs, (rows, span))
    lane_s = lax.broadcasted_iota(jnp.int32, (rows, span), 1)
    row_s = lax.broadcasted_iota(jnp.int32, (rows, span), 0)
    lane_p = lax.broadcasted_iota(jnp.int32, (rows, 128), 1)
    sign = jnp.where(lane_p % 64 < 32, -1.0, 1.0).astype(F32)

    def table_step(j, c):
        place = row_s + j * rows
        column = jnp.sum(jnp.where(lane_s == place, seg_all, 0.0), axis=1, keepdims=True)
        same = seg_all == column
        bias[j] = jnp.where(same, 0.0, -1e30).astype(F32)
        position = jnp.sum(jnp.where(same & (lane_s < place), 1.0, 0.0), axis=1, keepdims=True)
        angle = position * freq_ref[...]
        cosb[j] = jnp.cos(angle)
        sinb[j] = jnp.sin(angle) * sign
        return c

    lax.fori_loop(0, n_t, table_step, 0)

    gain1 = gain1_ref[...]
    gain2 = gain2_ref[...]

    def norm_step(i, c):
        j = visit(i)

        @pl.when(i == 1)
        def _():
            t_relay(0, xg)

        @pl.when(i > 1)
        def _():
            t_got(0, xg, j)

        unit, _ = rms_parts(xg[j].astype(F32))
        n1[j] = (unit * gain1).astype(BF)
        return c

    lax.fori_loop(0, n_t, norm_step, 0)

    def pass_on(stage, buf, z):
        p = 2 * z + xx
        d_got(stage, buf.at[wslice(p)], p)
        d_copy(stage, buf.at[wslice(p)], buf.at[wslice(p)], across, p, 5 + stage, p).start()

    def from_across(stage, buf):
        for z in range(n_z):
            p = 2 * z + 1 - xx
            d_got(stage, buf.at[wslice(p)], p)

    for z in z_peers:
        pass_on(0, ag, z)
    for z in z_peers:
        d_copy(1, b_ref, bg.at[wslice(d)], 2 * z + xx, d).start()
    d_copy(1, b_ref, bg.at[wslice(d)], across, d).start()
    from_across(0, ag)
    wo[...] = ag[:, qkv_cols:]

    def qkv_step(j, c):
        mixed = dot(n1[j], ag[:, :qkv_cols])
        cosine = cosb[j]
        sine = sinb[j]
        for k in range(2 * n_head // 2):
            chunk = mixed[:, 128 * k:128 * k + 128]
            chunk = chunk * cosine + partner(chunk) * sine
            for half in range(2):
                idx = 2 * k + half
                part = chunk[:, 64 * half:64 * half + 64]
                if idx < n_head:
                    part = part.astype(BF).astype(F32) * 0.125
                qkvh[idx, j] = part.astype(BF)
        for h in range(n_head):
            lo = 2 * head_cols + HD * h
            qkvh[2 * n_head + h, j] = mixed[:, lo:lo + HD].astype(BF)
        return c

    lax.fori_loop(0, n_t, qkv_step, 0)

    def attn_step(h, j, c):
        keys = qkvh[n_head + h].reshape(span, HD)
        vals = qkvh[2 * n_head + h].reshape(span, HD)
        s = dot(qkvh[h, j], keys, LAST) + bias[j]
        e = jnp.exp(s - jnp.max(s, axis=-1, keepdims=True))
        p = e * (1.0 / jnp.sum(e, axis=-1, keepdims=True))
        probs[h, j] = p
        hoh[h, j] = dot(p.astype(BF), vals).astype(BF)
        return c

    passed = 0
    for h in range(n_head):
        lax.fori_loop(0, n_t, functools.partial(attn_step, h), 0)
        until = n_z - 1 if h == n_head - 1 else min(passed + 1, n_z - 1)
        for z in z_peers[passed:until]:
            pass_on(1, bg, z)
        passed = until

    def send_part(stage, part, j, own, snd, rcv):
        @pl.when(j == t)
        def _():
            own[...] = part

        @pl.when(j != t)
        def _():
            snd[j] = part.astype(BF)
            t_copy(stage, snd.at[j], rcv.at[t], j, t).start()

    def order(i):
        return lax.rem(t + (2 + i) * (1 - i // 2) + (3 - i) * (i // 2), n_t)

    def attn_out_step(i, c):
        j = order(i)
        flat = jnp.concatenate([hoh[h, j] for h in range(n_head)], axis=1)
        hof[j] = flat
        send_part(2, dot(flat, wo[...], LAST), j, own1, rs1s, rs1r)
        return c

    lax.fori_loop(0, n_t, attn_out_step, 0)

    def collect(stage, own, rcv):
        total = own[...]
        for o in range(1, n_t):
            p = lax.rem(t + o, n_t)
            t_got(stage, rcv, p)
            total = total + rcv[p].astype(F32)
        return total

    from_across(1, bg)
    wg[...] = bg[:, :ff]
    wu[...] = bg[:, ff:2 * ff]
    wd[...] = bg[:, 2 * ff:3 * ff]

    def hidden_step(i, c):
        j = visit(i)

        @pl.when(i == 1)
        def _():
            t_relay(1, cg)

        @pl.when(i > 1)
        def _():
            t_got(1, cg, j)

        ghf[j] = dot(cg[j], wd[...])
        return c

    lax.fori_loop(0, n_t, hidden_step, 0)

    resid_mid = x_ref[...].astype(F32) + collect(2, own1, rs1r)
    mid[...] = resid_mid
    unit, inv2 = rms_parts(resid_mid)
    unit2[...] = unit
    n2g[t] = (unit * gain2).astype(BF)
    t_spread(3, n2g.at[t], n2g)

    def ffn_step(i, c):
        j = visit(i)

        @pl.when(i == 1)
        def _():
            t_relay(3, n2g)

        @pl.when(i > 1)
        def _():
            t_got(3, n2g, j)

        gate = dot(n2g[j], wg[...])
        up = dot(n2g[j], wu[...])
        cdf = 0.5 * (1.0 + lax.erf(gate * 0.7071067811865476))
        density = 0.3989422804014327 * jnp.exp(-0.5 * gate * gate)
        val = gate * cdf
        slope = cdf + gate * density
        hidden = (val * up).astype(BF)
        grad_hidden = ghf[j]
        m0 = (grad_hidden * up * slope).astype(BF)
        m1 = (grad_hidden * val).astype(BF)
        hid[j] = hidden
        mix0[j] = m0
        mix1[j] = m1
        send_part(4, dot(m0, wg[...], LAST) + dot(m1, wu[...], LAST), j, own2, rs2s, rs2r)
        send_part(5, dot(hidden, wd[...], LAST), j, own3, rs3s, rs3r)
        return c

    lax.fori_loop(0, n_t, ffn_step, 0)

    grad_two = collect(4, own2, rs2r)
    unit = unit2[...]
    gain_ffn_part = jnp.sum(grad_two * unit, axis=0, keepdims=True)
    grad_mid = cot_ref[...].astype(F32) + norm_back(grad_two, unit, inv2, gain2)
    gmid[...] = grad_mid
    gmg[t] = grad_mid.astype(BF)
    t_spread(6, gmg.at[t], gmg)

    def flat_cols(buf, lo, n):
        return buf[:, :, lo:lo + n].reshape(span, n)

    tile = 256
    hid_all = hid[...].reshape(span, ff)
    mix0_all = mix0[...].reshape(span, ff)
    mix1_all = mix1[...].reshape(span, ff)
    for lo in range(0, width, tile):
        lhs = flat_cols(n2g, lo, tile)
        bgs[lo:lo + tile, :ff] = dot(lhs, mix0_all, FIRST).astype(BF)
        bgs[lo:lo + tile, ff:2 * ff] = dot(lhs, mix1_all, FIRST).astype(BF)
        bgs[lo:lo + tile, 2 * ff:3 * ff] = dot(flat_cols(cg, lo, tile), hid_all, FIRST).astype(BF)
    bgs[:, 3 * ff:] = jnp.zeros((width, bgs.shape[1] - 3 * ff), BF)

    def reduce_across(stage, snd, rcv):
        for z in z_peers + [zz]:
            d_copy(stage, snd.at[wslice(2 * z + 1 - xx)], rcv.at[z], across, z, stage, z).start()

    def reduce_along(stage, snd, rcv, sums, got):
        for z in z_peers:
            d_got(stage, rcv.at[z], z)
            sums[z] = (snd[wslice(2 * z + xx), :].astype(F32) + rcv[z].astype(F32)).astype(BF)
            d_copy(stage + 5, sums.at[z], got.at[zz], 2 * z + xx, zz, stage + 5, z).start()

    def reduce_end(stage, snd, rcv, got):
        d_got(stage, rcv.at[zz], zz)
        total = snd[wslice(d), :].astype(F32) + rcv[zz].astype(F32)
        for z in z_peers:
            d_got(stage + 5, got.at[z], z)
            total = total + got[z].astype(F32)
        return total

    reduce_across(2, bgs, bxr)

    def grad_heads_step(i, c):
        j = visit(i)

        @pl.when(i == 1)
        def _():
            t_relay(6, gmg)

        @pl.when(i > 1)
        def _():
            t_got(6, gmg, j)

        gh = dot(gmg[j], wo[...]).astype(BF)
        for h in range(n_head):
            ghh[h, j] = gh[:, HD * h:HD * h + HD]
        return c

    lax.fori_loop(0, n_t, grad_heads_step, 0)

    def attn_back(h, c):
        keys = qkvh[n_head + h].reshape(span, HD)
        vals = qkvh[2 * n_head + h].reshape(span, HD)

        def step(j, c2):
            gh = ghh[h, j]
            row_dot = jnp.sum(gh.astype(F32) * hoh[h, j].astype(F32), axis=-1, keepdims=True)
            ds = (probs[h, j] * (dot(gh, vals, LAST) - row_dot)).astype(BF)
            dsb[j] = ds
            dqkv[h, j] = dot(ds, keys) * 0.125
            return c2

        lax.fori_loop(0, n_t, step, 0)
        dk = dot(dsb[...].reshape(span, span), qkvh[h].reshape(span, HD), FIRST)
        dqkv[n_head + h] = dk.reshape(n_t, rows, HD)
        pb = probs[h].reshape(span, span).astype(BF)
        dv = dot(pb, ghh[h].reshape(span, HD), FIRST)
        dqkv[2 * n_head + h] = dv.reshape(n_t, rows, HD)
        return c

    lax.fori_loop(0, n_head, attn_back, 0)

    reduce_along(2, bgs, bxr, bzs, bzr)

    def unrotate_step(j, c):
        cosine = cosb[j]
        sine = sinb[j]
        parts = []
        for k in range(n_head):
            chunk = jnp.concatenate([dqkv[2 * k, j], dqkv[2 * k + 1, j]], axis=1)
            parts.append(chunk * cosine - partner(chunk) * sine)
        parts = parts + [dqkv[2 * n_head + h, j] for h in range(n_head)]
        gq[j] = jnp.concatenate(parts, axis=1).astype(BF)
        return c

    lax.fori_loop(0, n_t, unrotate_step, 0)

    gq_all = gq[...].reshape(span, qkv_cols)
    ho_all = hof[...].reshape(span, head_cols)
    for lo in range(0, width, tile):
        ags[lo:lo + tile, :qkv_cols] = dot(flat_cols(n1, lo, tile), gq_all, FIRST).astype(BF)
        ags[lo:lo + tile, qkv_cols:] = dot(flat_cols(gmg, lo, tile), ho_all, FIRST).astype(BF)
    reduce_across(3, ags, axr)

    def qkv_back_step(i, c):
        j = order(i)
        send_part(7, dot(gq[j], ag[:, :qkv_cols], LAST), j, own4, rs4s, rs4r)
        return c

    lax.fori_loop(0, n_t, qkv_back_step, 0)
    reduce_along(3, ags, axr, azs, azr)

    grad_one = collect(7, own4, rs4r)
    unit1, inv1 = rms_parts(x_ref[...].astype(F32))
    gain_attn_part = jnp.sum(grad_one * unit1, axis=0, keepdims=True)
    gpt[t] = jnp.concatenate([gain_attn_part, gain_ffn_part, jnp.zeros((6, width), F32)], axis=0)
    for o in range(1, n_t):
        t_copy(8, gpt.at[t], gpt.at[t], lax.rem(t + o, n_t), t).start()
    gin_ref[...] = gmid[...] + norm_back(grad_one, unit1, inv1, gain1)
    out_ref[...] = (mid[...] + collect(5, own3, rs3r)).astype(BF)

    for o in range(1, n_t):
        t_got(8, gpt, lax.rem(t + o, n_t))
    gpd[d] = jnp.sum(gpt[...], axis=0)
    for o in range(1, n_dp):
        d_copy(4, gpd.at[d], gpd.at[d], lax.rem(d + o, n_dp), d).start()

    total = reduce_end(2, bgs, bxr, bzr)
    gin_w_ref[0] = total[:, :ff]
    gin_w_ref[1] = total[:, ff:2 * ff]
    gdown_ref[...] = total[:, 2 * ff:3 * ff]
    total = reduce_end(3, ags, axr, azr)
    for k in range(3):
        gqkv_ref[k] = total[:, head_cols * k:head_cols * (k + 1)]
    gwo_ref[...] = total[:, qkv_cols:]

    for o in range(1, n_dp):
        p = lax.rem(d + o, n_dp)
        d_got(4, gpd.at[p], p)
    gains = jnp.sum(gpd[...], axis=0)
    gain1_out[...] = gains[0:1]
    gain2_out[...] = gains[1:2]

    for o in range(1, n_t):
        p = lax.rem(t + o, n_t)
        for stage, ref in ((2, rs1s), (4, rs2s), (5, rs3s), (7, rs4s), (8, gpt)):
            t_copy(stage, ref.at[p], ref.at[p], p, p).wait_send()
    for stage, ref in ((0, xg), (1, cg), (3, n2g), (6, gmg)):
        for at in (over, other, t):
            t_copy(stage, ref.at[over], ref.at[over], other, over, at).wait_send()

    def d_sent(lane, ref, at):
        d_copy(0, ref, ref, across, d, lane, at).wait_send()

    for o in range(1, n_dp):
        d_sent(4, gpd.at[d], lax.rem(d + o, n_dp))
    for lane, own, part, sums in ((0, a_ref, axr, azs), (1, b_ref, bxr, bzs)):
        d_sent(lane, own, across)
        for z in z_peers:
            d_sent(lane, own, 2 * z + xx)
            d_sent(lane + 5, own, 2 * z + xx)
            d_sent(8 - lane, sums.at[z], z)
        for z in range(n_z):
            d_sent(3 - lane, part.at[z], z)


def on_device_fused(
    n_dp, n_t,
    inputs, segment_ids, gain_attn, gain_ffn, query_key_value_weight, w_out, w_ffn_in, w_ffn_out, cotangent,
):
    rows, width = inputs.shape
    wrows = w_out.shape[0]
    head_cols = w_out.shape[1]
    ff = w_ffn_out.shape[1]
    if n_t != 4 or n_dp % 2 or wrows % 16 or rows % 128 or head_cols % HD:
        return on_device(
            inputs, segment_ids, gain_attn, gain_ffn, query_key_value_weight, w_out, w_ffn_in, w_ffn_out, cotangent
        )
    n_head = head_cols // HD
    span = n_t * rows
    a_cols = 4 * head_cols
    b_cols = -(-3 * ff // 128) * 128
    half = np.arange(32, dtype=np.float64)
    freq = np.tile(THETA ** (-2.0 * half / HD), 4).astype(np.float32)[None]
    vmem = pl.BlockSpec(memory_space=pltpu.VMEM)
    act = (n_t, rows, width)

    part_a = (n_dp // 2, wrows, a_cols)
    part_b = (n_dp // 2, wrows, b_cols)

    def v(shape, kind=BF):
        return pltpu.VMEM(shape, kind)

    scratch = [
        v(act), v(act), v((width, a_cols)), v((width, b_cols)), v(act), v(act), v(act),
        v((n_t, rows, 128), F32), v((n_t, rows, 128), F32), v((n_t, rows, span), F32),
        v((3 * n_head, n_t, rows, HD)), v((n_head, n_t, rows, span), F32), v((n_head, n_t, rows, HD)),
        v((n_t, rows, head_cols)), v((width, head_cols)), v((width, ff)), v((width, ff)), v((width, ff)),
        v(act), v(act), v(act), v(act), v(act), v(act), v(act), v(act),
        v((rows, width), F32), v((rows, width), F32), v((rows, width), F32), v((rows, width), F32),
        v((n_t, rows, ff), F32), v((n_t, rows, ff)), v((n_t, rows, ff)), v((n_t, rows, ff)),
        v((rows, width), F32), v((rows, width), F32), v((rows, width), F32),
        v((n_head, n_t, rows, HD)), v((n_t, rows, span)), v((3 * n_head, n_t, rows, HD), F32),
        v((n_t, rows, 3 * head_cols)),
        v((width, a_cols)), v(part_a), v(part_a), v(part_a), v((width, b_cols)), v(part_b), v(part_b), v(part_b),
        v((n_t, 8, width), F32), v((n_dp, 8, width), F32), v((wrows, a_cols)), v((wrows, b_cols)),
        pltpu.SemaphoreType.DMA((9, n_t)), pltpu.SemaphoreType.DMA((9, n_t)),
        pltpu.SemaphoreType.DMA((9, n_dp)), pltpu.SemaphoreType.DMA((9, n_dp)),
    ]
    result, grad_input, gain_one, gain_two, grad_qkv, grad_out, grad_in, grad_down = pl.pallas_call(
        functools.partial(fused_kernel, n_dp, n_t, n_head, ff),
        out_shape=(
            jax.ShapeDtypeStruct((rows, width), BF),
            jax.ShapeDtypeStruct((rows, width), F32),
            jax.ShapeDtypeStruct((1, width), F32),
            jax.ShapeDtypeStruct((1, width), F32),
            jax.ShapeDtypeStruct((3, wrows, head_cols), F32),
            jax.ShapeDtypeStruct((wrows, head_cols), F32),
            jax.ShapeDtypeStruct((2, wrows, ff), F32),
            jax.ShapeDtypeStruct((wrows, ff), F32),
        ),
        in_specs=[vmem] * 10,
        out_specs=(vmem,) * 8,
        scratch_shapes=scratch,
        compiler_params=pltpu.CompilerParams(
            collective_id=0, has_side_effects=True, vmem_limit_bytes=60 * 1024 * 1024
        ),
        name="fused_layer",
    )(
        inputs, cotangent, segment_ids, gain_attn[None], gain_ffn[None], jnp.asarray(freq),
        jnp.swapaxes(query_key_value_weight, 0, 1), w_out, jnp.swapaxes(w_ffn_in, 0, 1), w_ffn_out,
    )
    return (
        result,
        grad_input,
        gain_one[0],
        gain_two[0],
        jnp.swapaxes(grad_qkv, 0, 1),
        grad_out,
        jnp.swapaxes(grad_in, 0, 1),
        grad_down,
    )


def solution(mesh):
    return jax.shard_map(
        functools.partial(on_device_fused, mesh.shape["dp"], mesh.shape["tensor"]),
        mesh=mesh,
        in_specs=(
            P(("dp", "tensor"), None),
            P("dp", None),
            P(),
            P(),
            P("dp", None, "tensor"),
            P("dp", "tensor"),
            P("dp", None, "tensor"),
            P("dp", "tensor"),
            P(("dp", "tensor"), None),
        ),
        out_specs=(
            P(("dp", "tensor"), None),
            P(("dp", "tensor"), None),
            P(),
            P(),
            P("dp", None, "tensor"),
            P("dp", "tensor"),
            P("dp", None, "tensor"),
            P("dp", "tensor"),
        ),
        check_vma=False,
    )
```
